256 devices in a mesh: rad: 16 (over y, x), azi: 16 (over z, core).
Axes of the slice: x: 4, y: 4, z: 8, core: 2. Of those that a mesh axis runs over, the one named last changes fastest.
Arguments:
- relative_base_heat: float32 [256, 512, 512], P('rad', 'azi'), may hold values from 0.75 to 1.25
- base_deformation_size: float32 [256, 512, 512], P('rad', 'azi'), may hold values from 0.25 to 1
- base_streamwise_flux: float32 [256, 512, 512], P('rad', 'azi'), may hold values from 0.2 to 1
- goal_heat_change: float32 [256, 512, 512], P('rad', 'azi'), may hold values from 0.25 to 2
- initial_costate_heat: float32 [256, 512, 512], P('rad', 'azi'), may hold values from 0.2 to 2
Outputs:
- temperature_adjoint: float32 [256, 512, 512], P('rad', 'azi')
- lengthwise_velocity_sensitivity: float32 [256, 512, 512], P('rad', 'azi')
The draws below stay inside these ranges and needn't reach their ends.
All inputs are finite; a program needn't handle non-finite values.
Results may differ from the reference program's by a relative error of at most 0.00045.
Values sent between devices are 32-bit elements; how exact they have to be, the bound alone decides.
No kernel may reach another device: no remote copies, remote signals or barrier semaphores. Data moves between devices by JAX's collectives and lax.ppermute only.
A program may use at most 128 MiB of HBM per device.

```python
import math
import jax
import jax.numpy as jnp
from jax import lax

NRD = 16
STREAMWISE_CUTS = 512
THICKNESS_CUTS = 256
CIRCUMFERENTIAL = 512


def block_levels(own_key, extent, cuts, low, high):
    loudness, own = 1.0, jax.random.fold_in(own_key, 6)
    for position, blocks in cuts:
        steps = jnp.exp(jax.random.uniform(jax.random.fold_in(own, position), (blocks,), jnp.float32, low / len(cuts), high / len(cuts)))
        loudness = loudness * jnp.repeat(steps, extent[position] // blocks).reshape([-1 if axis == position else 1 for axis in range(len(extent))])
    return loudness


def setup_inputs(seed: int = 0) -> dict:
    streams_of = jax.random.split(jax.random.key(seed), 6)
    relative_base_heat = jnp.clip(0.75 + 0.5 * jax.random.uniform(streams_of[0], (THICKNESS_CUTS, CIRCUMFERENTIAL, STREAMWISE_CUTS), jnp.float32) ** block_levels(streams_of[0], (THICKNESS_CUTS, CIRCUMFERENTIAL, STREAMWISE_CUTS), ((0, 16), (1, 16)), -0.2, 0.2), 0.75, 1.25)
    base_deformation_size = jnp.clip(jnp.exp(math.log(1.0) - 1.3862944 * jax.random.uniform(streams_of[1], (THICKNESS_CUTS, CIRCUMFERENTIAL, STREAMWISE_CUTS), jnp.float32) ** block_levels(streams_of[1], (THICKNESS_CUTS, CIRCUMFERENTIAL, STREAMWISE_CUTS), ((0, 16), (1, 16)), -0.2, 0.2)), 0.25, 1.0)
    base_streamwise_flux = jnp.clip(0.2 + 0.8 * jax.random.uniform(streams_of[2], (THICKNESS_CUTS, CIRCUMFERENTIAL, STREAMWISE_CUTS), jnp.float32) ** block_levels(streams_of[2], (THICKNESS_CUTS, CIRCUMFERENTIAL, STREAMWISE_CUTS), ((0, 16), (1, 16)), -0.2, 0.2), 0.2, 1.0)
    goal_heat_change = jnp.clip(jnp.exp(math.log(2.0) - 2.0794415 * jax.random.uniform(streams_of[3], (THICKNESS_CUTS, CIRCUMFERENTIAL, STREAMWISE_CUTS), jnp.float32) ** block_levels(streams_of[3], (THICKNESS_CUTS, CIRCUMFERENTIAL, STREAMWISE_CUTS), ((0, 16), (1, 16)), -0.2, 0.2)), 0.25, 2.0)
    initial_costate_heat = jnp.clip(jnp.exp(math.log(2.0) - 2.3025851 * jax.random.uniform(streams_of[4], (THICKNESS_CUTS, CIRCUMFERENTIAL, STREAMWISE_CUTS), jnp.float32) ** block_levels(streams_of[4], (THICKNESS_CUTS, CIRCUMFERENTIAL, STREAMWISE_CUTS), ((0, 16), (1, 16)), -0.2, 0.2)), 0.2, 2.0)
    return {"relative_base_heat": relative_base_heat, "base_deformation_size": base_deformation_size, "base_streamwise_flux": base_streamwise_flux, "goal_heat_change": goal_heat_change, "initial_costate_heat": initial_costate_heat}


radial_weight = 8.0
azimuth_weight = 0.25
axial_weight = 0.25
flow_weight = 0.5
mass_weight = 1.0
heat_weight = 0.25
arrhenius_exponent = 2.0
slope_weight = 2.0


def line_geometry(first_row, number_lines_total, total_rows, segment_rows):
    row_int = jnp.arange(number_lines_total, dtype=jnp.int32) + first_row
    row_float = row_int.astype(jnp.float32)
    total_float = float(total_rows)
    segment_float = float(segment_rows)
    radius = 1.0 + (row_float + 0.5) / total_float
    inner_face = 1.0 + row_float / total_float
    outer_face = 1.0 + (row_float + 1.0) / total_float
    stiffness = radial_weight * segment_float * segment_float
    lower_off = jnp.where(row_int == 0, 0.0, -stiffness * inner_face / radius)
    upper_off = jnp.where(row_int == total_rows - 1, 0.0, -stiffness * outer_face / radius)
    radial_diag = stiffness * (inner_face + outer_face) / radius
    azimuth_coef = azimuth_weight / (radius * radius)
    return lower_off, upper_off, radial_diag, azimuth_coef


def plate_arrays(relative_base_heat, base_deformation_size, base_streamwise_flux):
    polymer_resistance = jnp.exp(-arrhenius_exponent * (relative_base_heat - 1.0))
    heating = heat_weight * arrhenius_exponent * polymer_resistance * base_deformation_size * base_deformation_size
    transport_factor = flow_weight * base_streamwise_flux
    extra_pivot_entry = mass_weight + 2.0 * axial_weight + transport_factor + heating
    return polymer_resistance, transport_factor, extra_pivot_entry


def explicit_rhs(old_center, side_sum, azimuth_coef, transport_factor, source_field):
    edge_nulls = jnp.zeros_like(old_center[:, :, :1])
    next_cell = jnp.concatenate([old_center[:, :, 1:], edge_nulls], axis=2)
    prev_cell = jnp.concatenate([edge_nulls, old_center[:, :, :-1]], axis=2)
    return (source_field + azimuth_coef[:, None, None] * side_sum + axial_weight * (prev_cell + next_cell)
            + transport_factor * next_cell + mass_weight * old_center)


def velocity_factor(relative_base_heat, polymer_resistance, base_deformation_size):
    edge_nulls = jnp.zeros_like(relative_base_heat[:, :, :1])
    resistance_derivative_array = jnp.concatenate([relative_base_heat[:, :, 1:] - relative_base_heat[:, :, :-1], edge_nulls], axis=2)
    return slope_weight * resistance_derivative_array - 2.0 * heat_weight * polymer_resistance * base_deformation_size


def thomas_lines(lower_off, diagonal, upper_off, right_side):
    def forward(carry_pair, row_items):
        running_g_term, running_h_term = carry_pair
        lower_row, diag_row, upper_row, right_row = row_items
        denominator = diag_row - lower_row * running_h_term
        new_g = (right_row - lower_row * running_g_term) / denominator
        new_h = upper_row / denominator
        return (new_g, new_h), (new_g, new_h)

    zero_plane = jnp.zeros_like(right_side[0])
    final_pair, eliminated = lax.scan(forward, (zero_plane, zero_plane), (lower_off, diagonal, upper_off, right_side))

    def backward(carry_next, row_items):
        solved_row = row_items[0] - row_items[1] * carry_next
        return solved_row, solved_row

    last_row, solved = lax.scan(backward, zero_plane, eliminated, reverse=True)
    return solved


def reference(relative_base_heat, base_deformation_size, base_streamwise_flux, goal_heat_change, initial_costate_heat):
    lower_off, upper_off, radial_diag, azimuth_coef = line_geometry(0, THICKNESS_CUTS, THICKNESS_CUTS, NRD)
    polymer_resistance, transport_factor, extra_pivot_entry = plate_arrays(relative_base_heat, base_deformation_size, base_streamwise_flux)
    diagonal = radial_diag[:, None, None] + 2.0 * azimuth_coef[:, None, None] + extra_pivot_entry
    sequence_ordinal = initial_costate_heat
    for sweep_index in range(2):
        side_sum = jnp.roll(sequence_ordinal, 1, axis=1) + jnp.roll(sequence_ordinal, -1, axis=1)
        right_side = explicit_rhs(sequence_ordinal, side_sum, azimuth_coef, transport_factor, goal_heat_change)
        sequence_ordinal = thomas_lines(lower_off, diagonal, upper_off, right_side)
    lengthwise_velocity_sensitivity = sequence_ordinal * velocity_factor(relative_base_heat, polymer_resistance, base_deformation_size)
    return sequence_ordinal, lengthwise_velocity_sensitivity
```

```python
import jax
import jax.numpy as jnp
from jax import lax
from jax.experimental import pallas as pl
from jax.experimental.pallas import tpu as pltpu
from jax.sharding import PartitionSpec as P

radial_weight = 8.0
azimuth_weight = 0.25
axial_weight = 0.25
flow_weight = 0.5
mass_weight = 1.0
heat_weight = 0.25
arrhenius_exponent = 2.0
slope_weight = 2.0

SUB, LANE = 8, 128
F32 = jnp.float32


def geometry(rows):
    total = rows * lax.axis_size("rad")
    stiffness = radial_weight * rows * rows
    first = (lax.axis_index("rad") * rows).astype(F32)
    links = [stiffness + (stiffness / total) * (first + float(i)) for i in range(rows + 1)]
    radii = [1.0 + (first + (i + 0.5)) * (1.0 / total) for i in range(rows)]
    return links, radii


def splat(scalar):
    return jnp.full((1, LANE), scalar, F32)


def wide(row, width):
    return jnp.concatenate([row] * (width // LANE), axis=1)


def tiles_of(ref, group, plane, width):
    per = width // LANE
    return jnp.concatenate([ref[group * per + t, plane] for t in range(per)], axis=1)


def put_tiles(ref, group, plane, value):
    per = value.shape[1] // LANE
    for t in range(per):
        ref[group * per + t, plane] = value[:, t * LANE : (t + 1) * LANE]


def lane_next(value):
    width = value.shape[1]
    lane = lax.broadcasted_iota(jnp.int32, value.shape, 1)
    return jnp.where(lane == width - 1, 0.0, pltpu.roll(value, width - 1, 1))


def lane_prev(value):
    lane = lax.broadcasted_iota(jnp.int32, value.shape, 1)
    return jnp.where(lane == 0, 0.0, pltpu.roll(value, 1, 1))


def matrix_kernel(heat, deform, flux, ratio, left_map, right_map, factor, condensed):
    rows, azimuths, width = heat.shape
    links, radii = geometry(rows)
    inverse_links = [wide(1.0 / splat(link), width) for link in links]
    shunts = []
    for radius in radii:
        r = splat(radius)
        shunts.append(wide(2.0 * azimuth_weight / (r * r) + (mass_weight + 2.0 * axial_weight), width))
    for group in range(azimuths // SUB):
        here = pl.ds(group * SUB, SUB)
        ratios, lefts = [], []
        pivot = None
        through = jnp.full((SUB, width), links[0], F32)
        for i in range(rows):
            hot = heat[i, here, :]
            size = deform[i, here, :]
            drag = jnp.exp(-arrhenius_exponent * (hot - 1.0)) * size
            shunt = radii[i] * (
                shunts[i]
                + flow_weight * flux[i, here, :]
                + (heat_weight * arrhenius_exponent) * (drag * size)
            )
            lane = lax.broadcasted_iota(jnp.int32, hot.shape, 1)
            rise = jnp.where(lane == width - 1, 0.0, pltpu.roll(hot, width - 1, 1) - hot)
            factor[i, here, :] = slope_weight * rise - (2.0 * heat_weight) * drag
            pivot = shunt + (links[0] if i == 0 else ratios[-1] * pivot)
            lefts.append(through)
            if i < rows - 1:
                step = links[i + 1] / (links[i + 1] + pivot)
                ratios.append(step)
                ratio[i, here, :] = step
                through = step * through
        put_tiles(condensed, group, 0, through)
        put_tiles(condensed, group, 2, pivot)
        from_left = jnp.zeros((SUB, width), F32)
        from_right = jnp.ones((SUB, width), F32)
        left_map[rows - 1, here, :] = from_left
        right_map[rows - 1, here, :] = from_right
        ratio[rows - 1, here, :] = from_left
        for i in range(rows - 2, -1, -1):
            from_left = ratios[i] * (lefts[i] * inverse_links[i + 1] + from_left)
            from_right = ratios[i] * from_right
            left_map[i, here, :] = from_left
            right_map[i, here, :] = from_right
        put_tiles(condensed, group, 1, links[0] * (1.0 - from_left))


def sources(group, old, below, above, flux, goal, radii, quarter):
    rows, azimuths, width = old.shape
    here = pl.ds(group * SUB, SUB)
    sub = lax.broadcasted_iota(jnp.int32, (SUB, width), 0)
    out = []
    for i in range(rows):
        centre = old[i, here, :]
        low = below[i : i + 1, :] if group == 0 else old[i, group * SUB - 1 : group * SUB, :]
        high = (
            above[i : i + 1, :]
            if group == azimuths // SUB - 1
            else old[i, (group + 1) * SUB : (group + 1) * SUB + 1, :]
        )
        side = jnp.where(sub == 0, low, pltpu.roll(centre, 1, 0)) + jnp.where(
            sub == SUB - 1, high, pltpu.roll(centre, SUB - 1, 0)
        )
        after = lane_next(centre)
        right = (
            goal[i, here, :]
            + axial_weight * (lane_prev(centre) + after)
            + flow_weight * flux[i, here, :] * after
            + mass_weight * centre
        )
        out.append(radii[i] * right + quarter[i] * side)
    return out


def local_solve(group, source, ratio, inverse_links, particular):
    rows = len(source)
    here = pl.ds(group * SUB, SUB)
    ratios = [ratio[i, here, :] for i in range(rows - 1)]
    currents = [source[0]]
    for i in range(1, rows):
        currents.append(source[i] + ratios[i - 1] * currents[-1])
    value = jnp.zeros_like(source[0])
    particular[rows - 1, here, :] = value
    for i in range(rows - 2, -1, -1):
        value = ratios[i] * (currents[i] * inverse_links[i + 1] + value)
        particular[i, here, :] = value
    return value, currents[-1]


def tables(rows, width):
    links, radii = geometry(rows)
    inverse_links = [wide(1.0 / splat(link), width) for link in links]
    quarter = [wide(azimuth_weight / splat(radius), width) for radius in radii]
    return links, radii, inverse_links, quarter


def first_kernel(old, below, above, flux, goal, ratio, condensed, particular, message):
    rows, azimuths, width = old.shape
    links, radii, inverse_links, quarter = tables(rows, width)
    message[:, 0:3] = condensed[...]
    for group in range(azimuths // SUB):
        source = sources(group, old, below, above, flux, goal, radii, quarter)
        inner, outer = local_solve(group, source, ratio, inverse_links, particular)
        put_tiles(message, group, 3, links[0] * inner)
        put_tiles(message, group, 4, outer)


def reduced_kernel(rows, got, sent):
    segments = got.shape[0]
    last_link = 2.0 * radial_weight * rows * rows
    inverses, ratios, offsets = [], [], []
    for s in range(segments):
        diagonal = got[s, 2] + (got[s + 1, 1] if s + 1 < segments else last_link)
        right = got[s, 4] + (got[s + 1, 3] if s + 1 < segments else 0.0)
        if s > 0:
            diagonal = diagonal - got[s, 0] * ratios[-1]
            right = right + ratios[-1] * carried
        carried = right
        inverse = 1.0 / diagonal
        inverses.append(inverse)
        offsets.append(right * inverse)
        if s + 1 < segments:
            ratios.append(got[s + 1, 0] * inverse)
    zero = jnp.zeros_like(inverses[0])
    for s in range(segments - 1, -1, -1):
        if s + 1 < segments:
            value = offsets[s] + ratios[s] * value
            green = inverses[s] + ratios[s] * ratios[s] * green
            rising = ratios[s] * rising
        else:
            value, green, rising = offsets[s], inverses[s], jnp.ones_like(zero)
        falling = green / rising
        for plane, item in enumerate((value, rising, falling)):
            sent[s, 2 * plane + 1] = item
            if s + 1 < segments:
                sent[s + 1, 2 * plane] = item
    for plane in range(3):
        sent[0, 2 * plane] = zero


def second_kernel(particular, left_map, right_map, got, new, low_edge, high_edge):
    rows, azimuths, width = particular.shape
    for group in range(azimuths // SUB):
        here = pl.ds(group * SUB, SUB)
        left = tiles_of(got, group, 0, width)
        right = tiles_of(got, group, 1, width)
        for i in range(rows):
            value = particular[i, here, :] + left_map[i, here, :] * left + right_map[i, here, :] * right
            new[i, here, :] = value
            if group == 0:
                low_edge[i : i + 1, :] = value[0:1, :]
            if group == azimuths // SUB - 1:
                high_edge[i : i + 1, :] = value[SUB - 1 : SUB, :]


def third_kernel(old, below, above, flux, goal, ratio, got, particular, message, own):
    rows, azimuths, width = old.shape
    links, radii, inverse_links, quarter = tables(rows, width)
    segments = message.shape[0]
    me = lax.axis_index("rad")
    for group in range(azimuths // SUB):
        here = pl.ds(group * SUB, SUB)
        source = sources(group, old, below, above, flux, goal, radii, quarter)
        inner, outer = local_solve(group, source, ratio, inverse_links, particular)
        inner = links[0] * inner
        upward = tiles_of(got, group, 2, width) * inner + tiles_of(got, group, 3, width) * outer
        downward = tiles_of(got, group, 4, width) * inner + tiles_of(got, group, 5, width) * outer
        own[0, here, :] = upward
        own[1, here, :] = downward
        for s in range(segments):
            message[s, here, :] = jnp.where(s > me, upward, downward)


def last_kernel(particular, left_map, right_map, factor, got, own, arrived, result, sensitivity):
    rows, azimuths, width = particular.shape
    segments = arrived.shape[0]
    me = lax.axis_index("rad")
    for group in range(azimuths // SUB):
        here = pl.ds(group * SUB, SUB)
        lower = jnp.zeros((SUB, width), F32)
        upper = jnp.zeros((SUB, width), F32)
        for s in range(segments):
            item = arrived[s, here, :]
            lower = lower + jnp.where(s < me, item, 0.0)
            upper = upper + jnp.where(s > me, item, 0.0)
        left = tiles_of(got, group, 4, width) * lower + tiles_of(got, group, 2, width) * (
            own[1, here, :] + upper
        )
        right = (
            tiles_of(got, group, 5, width) * (lower + own[0, here, :])
            + tiles_of(got, group, 3, width) * upper
        )
        for i in range(rows):
            value = particular[i, here, :] + left_map[i, here, :] * left + right_map[i, here, :] * right
            result[i, here, :] = value
            sensitivity[i, here, :] = value * factor[i, here, :]


def call(kernel, outs, *args, flops=1_000_000):
    moved = sum(4 * a.size for a in args) + sum(4 * o.size for o in outs)
    return pl.pallas_call(
        kernel,
        out_shape=outs,
        in_specs=[pl.BlockSpec(memory_space=pltpu.VMEM)] * len(args),
        out_specs=tuple([pl.BlockSpec(memory_space=pltpu.VMEM)] * len(outs)),
        compiler_params=pltpu.CompilerParams(vmem_limit_bytes=24 * 2**20),
        cost_estimate=pl.CostEstimate(flops=flops, bytes_accessed=moved, transcendentals=0),
    )(*args)


def swap_edges(low_edge, high_edge):
    count = lax.axis_size("azi")
    below = lax.ppermute(high_edge, "azi", [(i, (i + 1) % count) for i in range(count)])
    above = lax.ppermute(low_edge, "azi", [((i + 1) % count, i) for i in range(count)])
    return below, above


def exchange(value):
    return lax.all_to_all(value, "rad", 0, 0, tiled=True)


def body(heat, deform, flux, goal, start):
    rows, azimuths, width = heat.shape
    segments = lax.axis_size("rad")
    tiles = azimuths * width // (SUB * LANE)
    block = jax.ShapeDtypeStruct((rows, azimuths, width), F32)
    edge = jax.ShapeDtypeStruct((rows, width), F32)

    def planes(count):
        return jax.ShapeDtypeStruct((tiles, count, SUB, LANE), F32)

    below, above = swap_edges(start[:, 0, :], start[:, azimuths - 1, :])
    ratio, left_map, right_map, factor, condensed = call(
        matrix_kernel, (block, block, block, block, planes(3)), heat, deform, flux, flops=20_000_000
    )
    particular, message = call(
        first_kernel, (block, planes(5)), start, below, above, flux, goal, ratio, condensed
    )
    sent = call(
        lambda got, sent: reduced_kernel(rows, got, sent),
        (jax.ShapeDtypeStruct((segments, 6, SUB, LANE), F32),),
        exchange(message),
    )[0]
    got = exchange(sent)
    new, low_edge, high_edge = call(
        second_kernel, (block, edge, edge), particular, left_map, right_map, got
    )
    below, above = swap_edges(low_edge, high_edge)
    particular, message, own = call(
        third_kernel,
        (
            block,
            jax.ShapeDtypeStruct((segments, azimuths, width), F32),
            jax.ShapeDtypeStruct((2, azimuths, width), F32),
        ),
        new,
        below,
        above,
        flux,
        goal,
        ratio,
        got,
    )
    arrived = exchange(message)
    return call(
        last_kernel, (block, block), particular, left_map, right_map, factor, got, own, arrived
    )


def solution(mesh):
    spec = P("rad", "azi", None)
    return jax.shard_map(
        body, mesh=mesh, in_specs=(spec,) * 5, out_specs=(spec, spec), check_vma=False
    )
```

```python
import jax
import jax.numpy as jnp
from jax import lax
from jax.experimental import pallas as pl
from jax.experimental.pallas import tpu as pltpu
from jax.sharding import PartitionSpec as P

radial_weight = 8.0
azimuth_weight = 0.25
axial_weight = 0.25
flow_weight = 0.5
mass_weight = 1.0
heat_weight = 0.25
arrhenius_exponent = 2.0
slope_weight = 2.0

SUB, LANE = 8, 128
GROUP = 4
F32 = jnp.float32


def geometry(rows):
    total = rows * lax.axis_size("rad")
    stiffness = radial_weight * rows * rows
    first = (lax.axis_index("rad") * rows).astype(F32)
    links = [stiffness + (stiffness / total) * (first + float(i)) for i in range(rows + 1)]
    radii = [1.0 + (first + (i + 0.5)) * (1.0 / total) for i in range(rows)]
    return links, radii


def splat(scalar):
    return jnp.full((1, LANE), scalar, F32)


def wide(row, width):
    return jnp.concatenate([row] * (width // LANE), axis=1)


def tiles_of(ref, group, plane, width):
    per = width // LANE
    return jnp.concatenate([ref[group * per + t, plane] for t in range(per)], axis=1)


def put_tiles(ref, group, plane, value):
    per = value.shape[1] // LANE
    for t in range(per):
        ref[group * per + t, plane] = value[:, t * LANE : (t + 1) * LANE]


def lane_next(value):
    width = value.shape[1]
    lane = lax.broadcasted_iota(jnp.int32, value.shape, 1)
    return jnp.where(lane == width - 1, 0.0, pltpu.roll(value, width - 1, 1))


def lane_prev(value):
    lane = lax.broadcasted_iota(jnp.int32, value.shape, 1)
    return jnp.where(lane == 0, 0.0, pltpu.roll(value, 1, 1))


def matrix_kernel(heat, deform, flux, ratio, left_map, right_map, factor, condensed):
    rows, azimuths, width = heat.shape
    links, radii = geometry(rows)
    inverse_links = [wide(1.0 / splat(link), width) for link in links]
    shunts = []
    for radius in radii:
        r = splat(radius)
        shunts.append(wide(2.0 * azimuth_weight / (r * r) + (mass_weight + 2.0 * axial_weight), width))
    for group in range(azimuths // SUB):
        here = pl.ds(group * SUB, SUB)
        ratios, lefts = [], []
        pivot = None
        through = jnp.full((SUB, width), links[0], F32)
        for i in range(rows):
            hot = heat[i, here, :]
            size = deform[i, here, :]
            drag = jnp.exp(-arrhenius_exponent * (hot - 1.0)) * size
            shunt = radii[i] * (
                shunts[i]
                + flow_weight * flux[i, here, :]
                + (heat_weight * arrhenius_exponent) * (drag * size)
            )
            lane = lax.broadcasted_iota(jnp.int32, hot.shape, 1)
            rise = jnp.where(lane == width - 1, 0.0, pltpu.roll(hot, width - 1, 1) - hot)
            factor[i, here, :] = slope_weight * rise - (2.0 * heat_weight) * drag
            pivot = shunt + (links[0] if i == 0 else ratios[-1] * pivot)
            lefts.append(through)
            if i < rows - 1:
                step = links[i + 1] / (links[i + 1] + pivot)
                ratios.append(step)
                ratio[i, here, :] = step
                through = step * through
        put_tiles(condensed, group, 0, through)
        put_tiles(condensed, group, 2, pivot)
        from_left = jnp.zeros((SUB, width), F32)
        from_right = jnp.ones((SUB, width), F32)
        left_map[rows - 1, here, :] = from_left
        right_map[rows - 1, here, :] = from_right
        ratio[rows - 1, here, :] = from_left
        for i in range(rows - 2, -1, -1):
            from_left = ratios[i] * (lefts[i] * inverse_links[i + 1] + from_left)
            from_right = ratios[i] * from_right
            left_map[i, here, :] = from_left
            right_map[i, here, :] = from_right
        put_tiles(condensed, group, 1, links[0] * (1.0 - from_left))


def sources(group, old, below, above, flux, goal, radii, quarter):
    rows, azimuths, width = old.shape
    here = pl.ds(group * SUB, SUB)
    sub = lax.broadcasted_iota(jnp.int32, (SUB, width), 0)
    out = []
    for i in range(rows):
        centre = old[i, here, :]
        low = below[i : i + 1, :] if group == 0 else old[i, group * SUB - 1 : group * SUB, :]
        high = (
            above[i : i + 1, :]
            if group == azimuths // SUB - 1
            else old[i, (group + 1) * SUB : (group + 1) * SUB + 1, :]
        )
        side = jnp.where(sub == 0, low, pltpu.roll(centre, 1, 0)) + jnp.where(
            sub == SUB - 1, high, pltpu.roll(centre, SUB - 1, 0)
        )
        after = lane_next(centre)
        right = (
            goal[i, here, :]
            + axial_weight * (lane_prev(centre) + after)
            + flow_weight * flux[i, here, :] * after
            + mass_weight * centre
        )
        out.append(radii[i] * right + quarter[i] * side)
    return out


def local_solve(group, source, ratio, inverse_links, particular):
    rows = len(source)
    here = pl.ds(group * SUB, SUB)
    ratios = [ratio[i, here, :] for i in range(rows - 1)]
    currents = [source[0]]
    for i in range(1, rows):
        currents.append(source[i] + ratios[i - 1] * currents[-1])
    value = jnp.zeros_like(source[0])
    particular[rows - 1, here, :] = value
    for i in range(rows - 2, -1, -1):
        value = ratios[i] * (currents[i] * inverse_links[i + 1] + value)
        particular[i, here, :] = value
    return value, currents[-1]


def tables(rows, width):
    links, radii = geometry(rows)
    inverse_links = [wide(1.0 / splat(link), width) for link in links]
    quarter = [wide(azimuth_weight / splat(radius), width) for radius in radii]
    return links, radii, inverse_links, quarter


def first_kernel(old, below, above, flux, goal, ratio, condensed, particular, message):
    rows, azimuths, width = old.shape
    links, radii, inverse_links, quarter = tables(rows, width)
    message[:, 0:3] = condensed[...]
    for group in range(azimuths // SUB):
        source = sources(group, old, below, above, flux, goal, radii, quarter)
        inner, outer = local_solve(group, source, ratio, inverse_links, particular)
        put_tiles(message, group, 3, links[0] * inner)
        put_tiles(message, group, 4, outer)


def reduced_kernel(rows, got, sent):
    segments = got.shape[0]
    last_link = 2.0 * radial_weight * rows * rows
    inverses, ratios, offsets = [], [], []
    for s in range(segments):
        diagonal = got[s, 2] + (got[s + 1, 1] if s + 1 < segments else last_link)
        right = got[s, 4] + (got[s + 1, 3] if s + 1 < segments else 0.0)
        if s > 0:
            diagonal = diagonal - got[s, 0] * ratios[-1]
            right = right + ratios[-1] * carried
        carried = right
        inverse = 1.0 / diagonal
        inverses.append(inverse)
        offsets.append(right * inverse)
        if s + 1 < segments:
            ratios.append(got[s + 1, 0] * inverse)
    zero = jnp.zeros_like(inverses[0])
    for s in range(segments - 1, -1, -1):
        if s + 1 < segments:
            value = offsets[s] + ratios[s] * value
            green = inverses[s] + ratios[s] * ratios[s] * green
            rising = ratios[s] * rising
        else:
            value, green, rising = offsets[s], inverses[s], jnp.ones_like(zero)
        falling = green / rising
        for plane, item in enumerate((value, rising, falling)):
            sent[s, 2 * plane + 1] = item
            if s + 1 < segments:
                sent[s + 1, 2 * plane] = item
    for plane in range(3):
        sent[0, 2 * plane] = zero


def second_kernel(particular, left_map, right_map, got, new, low_edge, high_edge):
    rows, azimuths, width = particular.shape
    for group in range(azimuths // SUB):
        here = pl.ds(group * SUB, SUB)
        left = tiles_of(got, group, 0, width)
        right = tiles_of(got, group, 1, width)
        for i in range(rows):
            value = particular[i, here, :] + left_map[i, here, :] * left + right_map[i, here, :] * right
            new[i, here, :] = value
            if group == 0:
                low_edge[i : i + 1, :] = value[0:1, :]
            if group == azimuths // SUB - 1:
                high_edge[i : i + 1, :] = value[SUB - 1 : SUB, :]


def third_kernel(old, below, above, flux, goal, ratio, got, particular, own):
    rows, azimuths, width = old.shape
    links, radii, inverse_links, quarter = tables(rows, width)
    for group in range(azimuths // SUB):
        here = pl.ds(group * SUB, SUB)
        source = sources(group, old, below, above, flux, goal, radii, quarter)
        inner, outer = local_solve(group, source, ratio, inverse_links, particular)
        inner = links[0] * inner
        upward = tiles_of(got, group, 2, width) * inner + tiles_of(got, group, 3, width) * outer
        downward = tiles_of(got, group, 4, width) * inner + tiles_of(got, group, 5, width) * outer
        own[0, here, :] = upward
        own[1, here, :] = downward


def gather_kernel(own, first, second, third, near, message):
    mine = lax.rem(lax.axis_index("rad"), GROUP)
    block = lax.div(lax.axis_index("rad"), GROUP)
    for group in range(own.shape[1] // SUB):
        here = pl.ds(group * SUB, SUB)
        upward, downward = own[0, here, :], own[1, here, :]
        lower, upper = jnp.zeros_like(upward), downward
        for flip, other in ((1, first), (2, second), (3, third)):
            up, down = other[0, here, :], other[1, here, :]
            upward = upward + up
            downward = downward + down
            below = (mine ^ flip) < mine
            lower = lower + jnp.where(below, up, 0.0)
            upper = upper + jnp.where(below, 0.0, down)
        near[0, here, :] = lower
        near[1, here, :] = upper
        for slot, flip in ((0, 1), (1, 2)):
            message[slot, here, :] = jnp.where((block ^ flip) > block, upward, downward)


def last_kernel(
    particular, left_map, right_map, factor, got, own, near, first, second, third, result, sensitivity
):
    rows, azimuths, width = particular.shape
    block = lax.div(lax.axis_index("rad"), GROUP)
    for group in range(azimuths // SUB):
        here = pl.ds(group * SUB, SUB)
        lower, upper = near[0, here, :], near[1, here, :]
        for flip, other in ((1, first), (2, second), (3, third)):
            item = other[here, :]
            below = (block ^ flip) < block
            lower = lower + jnp.where(below, item, 0.0)
            upper = upper + jnp.where(below, 0.0, item)
        left = tiles_of(got, group, 4, width) * lower + tiles_of(got, group, 2, width) * upper
        right = (
            tiles_of(got, group, 5, width) * (lower + own[0, here, :])
            + tiles_of(got, group, 3, width) * (upper - own[1, here, :])
        )
        for i in range(rows):
            value = particular[i, here, :] + left_map[i, here, :] * left + right_map[i, here, :] * right
            result[i, here, :] = value
            sensitivity[i, here, :] = value * factor[i, here, :]


def call(kernel, outs, *args, flops=1_000_000):
    moved = sum(4 * a.size for a in args) + sum(4 * o.size for o in outs)
    return pl.pallas_call(
        kernel,
        out_shape=outs,
        in_specs=[pl.BlockSpec(memory_space=pltpu.VMEM)] * len(args),
        out_specs=tuple([pl.BlockSpec(memory_space=pltpu.VMEM)] * len(outs)),
        compiler_params=pltpu.CompilerParams(vmem_limit_bytes=24 * 2**20),
        cost_estimate=pl.CostEstimate(flops=flops, bytes_accessed=moved, transcendentals=0),
    )(*args)


def swap_edges(low_edge, high_edge):
    count = lax.axis_size("azi")
    below = lax.ppermute(high_edge, "azi", [(i, (i + 1) % count) for i in range(count)])
    above = lax.ppermute(low_edge, "azi", [((i + 1) % count, i) for i in range(count)])
    return below, above


def flip_permute(value, flip):
    return lax.ppermute(value, "rad", [(i, i ^ flip) for i in range(lax.axis_size("rad"))])


def exchange(value):
    return lax.all_to_all(value, "rad", 0, 0, tiled=True)


def body(heat, deform, flux, goal, start):
    rows, azimuths, width = heat.shape
    segments = lax.axis_size("rad")
    tiles = azimuths * width // (SUB * LANE)
    block = jax.ShapeDtypeStruct((rows, azimuths, width), F32)
    edge = jax.ShapeDtypeStruct((rows, width), F32)

    def planes(count):
        return jax.ShapeDtypeStruct((tiles, count, SUB, LANE), F32)

    below, above = swap_edges(start[:, 0, :], start[:, azimuths - 1, :])
    ratio, left_map, right_map, factor, condensed = call(
        matrix_kernel, (block, block, block, block, planes(3)), heat, deform, flux, flops=20_000_000
    )
    particular, message = call(
        first_kernel, (block, planes(5)), start, below, above, flux, goal, ratio, condensed
    )
    sent = call(
        lambda got, sent: reduced_kernel(rows, got, sent),
        (jax.ShapeDtypeStruct((segments, 6, SUB, LANE), F32),),
        exchange(message),
    )[0]
    got = exchange(sent)
    new, low_edge, high_edge = call(
        second_kernel, (block, edge, edge), particular, left_map, right_map, got
    )
    below, above = swap_edges(low_edge, high_edge)
    pair = jax.ShapeDtypeStruct((2, azimuths, width), F32)
    particular, own = call(third_kernel, (block, pair), new, below, above, flux, goal, ratio, got)
    others = [flip_permute(own, flip) for flip in (1, 2, 3)]
    near, message = call(gather_kernel, (pair, pair), own, *others)
    far = [flip_permute(message[min(flip, 2) - 1], flip * GROUP) for flip in (1, 2, 3)]
    return call(
        last_kernel,
        (block, block),
        particular,
        left_map,
        right_map,
        factor,
        got,
        own,
        near,
        *far,
    )


def solution(mesh):
    spec = P("rad", "azi", None)
    return jax.shard_map(
        body, mesh=mesh, in_specs=(spec,) * 5, out_specs=(spec, spec), check_vma=False
    )
```

```python
import jax
import jax.numpy as jnp
from jax import lax
from jax.experimental import pallas as pl
from jax.experimental.pallas import tpu as pltpu
from jax.sharding import PartitionSpec as P

radial_weight = 8.0
azimuth_weight = 0.25
axial_weight = 0.25
flow_weight = 0.5
mass_weight = 1.0
heat_weight = 0.25
arrhenius_exponent = 2.0
slope_weight = 2.0

SUB, LANE = 8, 128
GROUP = 4
F32 = jnp.float32


def geometry(rows):
    total = rows * lax.axis_size("rad")
    stiffness = radial_weight * rows * rows
    first = (lax.axis_index("rad") * rows).astype(F32)
    links = [stiffness + (stiffness / total) * (first + float(i)) for i in range(rows + 1)]
    radii = [1.0 + (first + (i + 0.5)) * (1.0 / total) for i in range(rows)]
    return links, radii


def splat(scalar):
    return jnp.full((1, LANE), scalar, F32)


def wide(row, width):
    return jnp.concatenate([row] * (width // LANE), axis=1)


def tiles_of(ref, group, plane, width):
    per = width // LANE
    return jnp.concatenate([ref[group * per + t, plane] for t in range(per)], axis=1)


def put_tiles(ref, group, plane, value):
    per = value.shape[1] // LANE
    for t in range(per):
        ref[group * per + t, plane] = value[:, t * LANE : (t + 1) * LANE]


def lane_next(value):
    width = value.shape[1]
    lane = lax.broadcasted_iota(jnp.int32, value.shape, 1)
    return jnp.where(lane == width - 1, 0.0, pltpu.roll(value, width - 1, 1))


def lane_prev(value):
    lane = lax.broadcasted_iota(jnp.int32, value.shape, 1)
    return jnp.where(lane == 0, 0.0, pltpu.roll(value, 1, 1))


def shunt_of(hot, size, drag_flux, radius, base):
    drag = jnp.exp(-arrhenius_exponent * (hot - 1.0)) * size
    heating = (heat_weight * arrhenius_exponent) * (drag * size)
    return drag, radius * (base + flow_weight * drag_flux + heating)


def ladder(shunts, links, inverse_links):
    rows = len(shunts)
    ratios, lefts = [], []
    through = jnp.full(shunts[0].shape, links[0], F32)
    pivot = shunts[0] + links[0]
    for i in range(rows):
        if i > 0:
            pivot = shunts[i] + ratios[-1] * pivot
        lefts.append(through)
        if i < rows - 1:
            step = links[i + 1] / (links[i + 1] + pivot)
            ratios.append(step)
            through = step * through
    from_left = jnp.zeros_like(through)
    from_right = jnp.ones_like(through)
    left_maps, right_maps = [from_left], [from_right]
    for i in range(rows - 2, -1, -1):
        from_left = ratios[i] * (lefts[i] * inverse_links[i + 1] + from_left)
        from_right = ratios[i] * from_right
        left_maps.append(from_left)
        right_maps.append(from_right)
    inner = links[0] * (1.0 - from_left)
    return ratios, left_maps[::-1], right_maps[::-1], (through, inner, pivot)


def base_shunts(radii):
    out = []
    for radius in radii:
        r = splat(radius)
        out.append(2.0 * azimuth_weight / (r * r) + (mass_weight + 2.0 * axial_weight))
    return out


def matrix_kernel(
    heat, deform, flux, ratio, left_map, right_map, factor, condensed, hot_in, size_in, flux_in, ready
):
    rows, azimuths, width = heat.shape
    groups = azimuths // SUB
    copies = []
    for group in range(groups):
        here = pl.ds(group * SUB, SUB)
        for k, (source, target) in enumerate(((heat, hot_in), (deform, size_in), (flux, flux_in))):
            copy = pltpu.make_async_copy(
                source.at[:, here, :], target.at[:, here, :], ready.at[group, k]
            )
            copy.start()
            copies.append(copy)
    links, radii = geometry(rows)
    inverse_links = [wide(1.0 / splat(link), width) for link in links]
    bases = [wide(base, width) for base in base_shunts(radii)]
    for group in range(groups):
        here = pl.ds(group * SUB, SUB)
        for copy in copies[3 * group : 3 * group + 3]:
            copy.wait()
        shunts = []
        for i in range(rows):
            hot = hot_in[i, here, :]
            drag, shunt = shunt_of(hot, size_in[i, here, :], flux_in[i, here, :], radii[i], bases[i])
            shunts.append(shunt)
            lane = lax.broadcasted_iota(jnp.int32, hot.shape, 1)
            rise = jnp.where(lane == width - 1, 0.0, pltpu.roll(hot, width - 1, 1) - hot)
            factor[i, here, :] = slope_weight * rise - (2.0 * heat_weight) * drag
        ratios, lefts, rights, ports = ladder(shunts, links, inverse_links)
        for i in range(rows):
            ratio[i, here, :] = ratios[i] if i < rows - 1 else jnp.zeros_like(hot)
            left_map[i, here, :] = lefts[i]
            right_map[i, here, :] = rights[i]
        for plane, port in enumerate(ports):
            put_tiles(condensed, group, plane, port)


def edge_kernel(heat, deform, flux, goal, old, low_edge, high_edge, held, ready):
    rows, azimuths, width = heat.shape
    spans = (pl.ds(0, SUB), pl.ds(azimuths - SUB, SUB))
    copies = []
    for k, source in enumerate((heat, deform, flux, goal, old)):
        for e in range(2):
            copy = pltpu.make_async_copy(source.at[:, spans[e], :], held.at[k, e], ready.at[k, e])
            copy.start()
            copies.append(copy)
    total = rows * lax.axis_size("rad")
    first = (lax.axis_index("rad") * rows).astype(F32)
    row = lax.broadcasted_iota(jnp.int32, (rows, width), 0).astype(F32)
    radius = 1.0 + (first + (row + 0.5)) * (1.0 / total)
    base = 2.0 * azimuth_weight / (radius * radius) + (mass_weight + 2.0 * axial_weight)
    quarter = azimuth_weight / radius
    for copy in copies:
        copy.wait()

    def line(k, e, at):
        return jnp.concatenate([held[k, e, i, at : at + 1, :] for i in range(rows)], axis=0)

    for e, (at, inner, out) in enumerate(((0, 1, low_edge), (SUB - 1, SUB - 2, high_edge))):
        moving = line(2, e, at)
        centre = line(4, e, at)
        _, shunt = shunt_of(line(0, e, at), line(1, e, at), moving, radius, base)
        out[0] = shunt
        out[1] = radius * explicit(centre, moving, line(3, e, at)) + quarter * line(4, e, inner)
        out[2] = centre


def explicit(centre, moving, given):
    after = lane_next(centre)
    return (
        given
        + axial_weight * (lane_prev(centre) + after)
        + flow_weight * moving * after
        + mass_weight * centre
    )


def sources(group, old, below, above, flux, goal, radii, quarter):
    rows, azimuths, width = old.shape
    here = pl.ds(group * SUB, SUB)
    sub = lax.broadcasted_iota(jnp.int32, (SUB, width), 0)
    out = []
    for i in range(rows):
        centre = old[i, here, :]
        low = below(i) if group == 0 else old[i, group * SUB - 1 : group * SUB, :]
        high = (
            above(i)
            if group == azimuths // SUB - 1
            else old[i, (group + 1) * SUB : (group + 1) * SUB + 1, :]
        )
        side = jnp.where(sub == 0, low, pltpu.roll(centre, 1, 0)) + jnp.where(
            sub == SUB - 1, high, pltpu.roll(centre, SUB - 1, 0)
        )
        right = explicit(centre, flux[i, here, :], goal[i, here, :])
        out.append(radii[i] * right + quarter[i] * side)
    return out


def substitute(source, ratios, inverse_links):
    rows = len(source)
    currents = [source[0]]
    for i in range(1, rows):
        currents.append(source[i] + ratios[i - 1] * currents[-1])
    value = jnp.zeros_like(source[0])
    values = [value]
    for i in range(rows - 2, -1, -1):
        value = ratios[i] * (currents[i] * inverse_links[i + 1] + value)
        values.append(value)
    return values[::-1], currents[-1]


def local_solve(group, source, ratio, inverse_links, particular):
    rows = len(source)
    here = pl.ds(group * SUB, SUB)
    ratios = [ratio[i, here, :] for i in range(rows - 1)]
    values, outer = substitute(source, ratios, inverse_links)
    for i in range(rows):
        particular[i, here, :] = values[i]
    return values[0], outer


def tables(rows, width):
    links, radii = geometry(rows)
    inverse_links = [wide(1.0 / splat(link), width) for link in links]
    quarter = [wide(azimuth_weight / splat(radius), width) for radius in radii]
    return links, radii, inverse_links, quarter


def pair_of(below, above):
    return jnp.concatenate([below, above], axis=0)


def first_kernel(
    old, below, above, flux, goal, ratio, condensed, particular, message, outside
):
    rows, azimuths, width = old.shape
    links, radii, inverse_links, quarter = tables(rows, width)
    tiles = message.shape[0]
    per = width // LANE
    message[:, 0:3] = condensed[...]
    message[:, 5] = jnp.ones((tiles, SUB, LANE), F32)

    shunts, source = [], []
    for i in range(rows):
        row = pl.ds(i, 1)
        shunts.append(pair_of(below[0, row, :], above[0, row, :]))
        beside = pair_of(old[i, 0:1, :], old[i, azimuths - 1 : azimuths, :])
        source.append(pair_of(below[1, row, :], above[1, row, :]) + quarter[i] * beside)
    ratios, lefts, rights, ports = ladder(shunts, links, inverse_links)
    values, outer = substitute(source, ratios, inverse_links)
    for i in range(rows):
        outside[0, i] = values[i]
        outside[1, i] = lefts[i]
        outside[2, i] = rights[i]
    for plane, port in enumerate((*ports, links[0] * values[0], outer)):
        for e in range(2):
            for t in range(per):
                message[e * per + t, 5, plane : plane + 1, :] = port[
                    e : e + 1, t * LANE : (t + 1) * LANE
                ]

    for group in range(azimuths // SUB):
        source = sources(
            group,
            old,
            lambda i: below[2, i : i + 1, :],
            lambda i: above[2, i : i + 1, :],
            flux,
            goal,
            radii,
            quarter,
        )
        inner, outer = local_solve(group, source, ratio, inverse_links, particular)
        put_tiles(message, group, 3, links[0] * inner)
        put_tiles(message, group, 4, outer)


def reduced_solve(last_link, through, inner, pivot, left, right):
    segments = len(through)
    inverses, ratios, offsets = [], [], []
    for s in range(segments):
        diagonal = pivot[s] + (inner[s + 1] if s + 1 < segments else last_link)
        given = right[s] + (left[s + 1] if s + 1 < segments else 0.0)
        if s > 0:
            diagonal = diagonal - through[s] * ratios[-1]
            given = given + ratios[-1] * carried
        carried = given
        inverse = 1.0 / diagonal
        inverses.append(inverse)
        offsets.append(given * inverse)
        if s + 1 < segments:
            ratios.append(through[s + 1] * inverse)
    out = []
    for s in range(segments - 1, -1, -1):
        if s + 1 < segments:
            value = offsets[s] + ratios[s] * value
            green = inverses[s] + ratios[s] * ratios[s] * green
            rising = ratios[s] * rising
        else:
            value, green, rising = offsets[s], inverses[s], jnp.ones_like(offsets[s])
        out.append((value, green, rising))
    return out[::-1]


def reduced_kernel(rows, got, sent):
    segments = got.shape[0]
    last_link = 2.0 * radial_weight * rows * rows
    main = reduced_solve(last_link, *[[got[s, p] for s in range(segments)] for p in range(5)])
    extra = reduced_solve(
        last_link, *[[got[s, 5, p : p + 1, :] for s in range(segments)] for p in range(5)]
    )
    zero = jnp.zeros((SUB, LANE), F32)
    for plane in range(3):
        sent[0, 2 * plane] = zero
    for s in range(segments):
        sent[s, 6] = zero
    for s in range(segments):
        value, green, rising = main[s]
        for plane, item in enumerate((value, rising, green / rising)):
            sent[s, 2 * plane + 1] = item
            if s + 1 < segments:
                sent[s + 1, 2 * plane] = item
        sent[s, 6, 1:2, :] = extra[s][0]
        if s + 1 < segments:
            sent[s + 1, 6, 0:1, :] = extra[s][0]


def third_kernel(
    before, left_map, right_map, outside, flux, goal, ratio, got, particular, own, new
):
    rows, azimuths, width = before.shape
    links, radii, inverse_links, quarter = tables(rows, width)
    per = width // LANE
    for group in range(azimuths // SUB):
        here = pl.ds(group * SUB, SUB)
        left = tiles_of(got, group, 0, width)
        right = tiles_of(got, group, 1, width)
        for i in range(rows):
            new[i, here, :] = (
                before[i, here, :] + left_map[i, here, :] * left + right_map[i, here, :] * right
            )

    def beyond(end):
        return pair_of(
            *[
                jnp.concatenate([got[e * per + t, 6, end : end + 1, :] for t in range(per)], axis=1)
                for e in range(2)
            ]
        )

    left, right = beyond(0), beyond(1)
    halo = [outside[0, i] + outside[1, i] * left + outside[2, i] * right for i in range(rows)]
    for group in range(azimuths // SUB):
        here = pl.ds(group * SUB, SUB)
        source = sources(
            group,
            new,
            lambda i: halo[i][0:1, :],
            lambda i: halo[i][1:2, :],
            flux,
            goal,
            radii,
            quarter,
        )
        inner, outer = local_solve(group, source, ratio, inverse_links, particular)
        inner = links[0] * inner
        own[0, here, :] = (
            tiles_of(got, group, 2, width) * inner + tiles_of(got, group, 3, width) * outer
        )
        own[1, here, :] = (
            tiles_of(got, group, 4, width) * inner + tiles_of(got, group, 5, width) * outer
        )


def gather_kernel(own, first, second, third, near, message):
    mine = lax.rem(lax.axis_index("rad"), GROUP)
    block = lax.div(lax.axis_index("rad"), GROUP)
    for group in range(own.shape[1] // SUB):
        here = pl.ds(group * SUB, SUB)
        upward, downward = own[0, here, :], own[1, here, :]
        lower, upper = jnp.zeros_like(upward), downward
        for flip, other in ((1, first), (2, second), (3, third)):
            up, down = other[0, here, :], other[1, here, :]
            upward = upward + up
            downward = downward + down
            below = (mine ^ flip) < mine
            lower = lower + jnp.where(below, up, 0.0)
            upper = upper + jnp.where(below, 0.0, down)
        near[0, here, :] = lower
        near[1, here, :] = upper
        for slot, flip in ((0, 1), (1, 2)):
            message[slot, here, :] = jnp.where((block ^ flip) > block, upward, downward)


def last_kernel(
    particular,
    left_map,
    right_map,
    factor,
    got,
    own,
    near,
    first,
    second,
    third,
    result,
    sensitivity,
    result_out,
    sensitivity_out,
    done,
):
    rows, azimuths, width = particular.shape
    block = lax.div(lax.axis_index("rad"), GROUP)
    copies = []
    for group in range(azimuths // SUB):
        here = pl.ds(group * SUB, SUB)
        lower, upper = near[0, here, :], near[1, here, :]
        for flip, other in ((1, first), (2, second), (3, third)):
            item = other[here, :]
            below = (block ^ flip) < block
            lower = lower + jnp.where(below, item, 0.0)
            upper = upper + jnp.where(below, 0.0, item)
        left = tiles_of(got, group, 4, width) * lower + tiles_of(got, group, 2, width) * upper
        right = (
            tiles_of(got, group, 5, width) * (lower + own[0, here, :])
            + tiles_of(got, group, 3, width) * (upper - own[1, here, :])
        )
        for i in range(rows):
            value = particular[i, here, :] + left_map[i, here, :] * left + right_map[i, here, :] * right
            result_out[i, here, :] = value
            sensitivity_out[i, here, :] = value * factor[i, here, :]
        for k, (source, target) in enumerate(((result_out, result), (sensitivity_out, sensitivity))):
            copy = pltpu.make_async_copy(
                source.at[:, here, :], target.at[:, here, :], done.at[group, k]
            )
            copy.start()
            copies.append(copy)
    for copy in copies:
        copy.wait()


def call(kernel, outs, *args, flops=1_000_000, remote=(), remote_outs=False, scratch=(), room=24):
    moved = sum(4 * a.size for a in args) + sum(4 * o.size for o in outs)
    near, away = pl.BlockSpec(memory_space=pltpu.VMEM), pl.BlockSpec(memory_space=pltpu.HBM)
    return pl.pallas_call(
        kernel,
        out_shape=outs,
        in_specs=[away if k in remote else near for k in range(len(args))],
        out_specs=tuple([away if remote_outs else near] * len(outs)),
        scratch_shapes=list(scratch),
        compiler_params=pltpu.CompilerParams(vmem_limit_bytes=room * 2**20),
        cost_estimate=pl.CostEstimate(flops=flops, bytes_accessed=moved, transcendentals=0),
    )(*args)


def swap_edges(low_edge, high_edge):
    count = lax.axis_size("azi")
    below = lax.ppermute(high_edge, "azi", [(i, (i + 1) % count) for i in range(count)])
    above = lax.ppermute(low_edge, "azi", [((i + 1) % count, i) for i in range(count)])
    return below, above


def flip_permute(value, flip):
    return lax.ppermute(value, "rad", [(i, i ^ flip) for i in range(lax.axis_size("rad"))])


def exchange(value):
    return lax.all_to_all(value, "rad", 0, 0, tiled=True)


def body(heat, deform, flux, goal, start):
    rows, azimuths, width = heat.shape
    segments = lax.axis_size("rad")
    groups = azimuths // SUB
    tiles = azimuths * width // (SUB * LANE)
    block = jax.ShapeDtypeStruct((rows, azimuths, width), F32)
    pair = jax.ShapeDtypeStruct((2, azimuths, width), F32)
    edge = jax.ShapeDtypeStruct((3, rows, width), F32)
    held = pltpu.VMEM((rows, azimuths, width), F32)

    def planes(count):
        return jax.ShapeDtypeStruct((tiles, count, SUB, LANE), F32)

    edges = call(
        edge_kernel,
        (edge, edge),
        heat,
        deform,
        flux,
        goal,
        start,
        remote=range(5),
        room=54,
scratch=(pltpu.VMEM((5, 2, rows, SUB, width), F32), pltpu.SemaphoreType.DMA((5, 2))),
    )
    below, above = swap_edges(*edges)
    ratio, left_map, right_map, factor, condensed = call(
        matrix_kernel,
        (block, block, block, block, planes(3)),
        heat,
        deform,
        flux,
        flops=20_000_000,
        remote=range(3),
        room=49,
        scratch=(held, held, held, pltpu.SemaphoreType.DMA((groups, 3))),
    )
    particular, message, outside = call(
        first_kernel,
        (block, planes(6), jax.ShapeDtypeStruct((3, rows, 2, width), F32)),
        start,
        below,
        above,
        flux,
        goal,
        ratio,
        condensed,
    )
    sent = call(
        lambda got, sent: reduced_kernel(rows, got, sent),
        (jax.ShapeDtypeStruct((segments, 7, SUB, LANE), F32),),
        exchange(message),
    )[0]
    got = exchange(sent)
    particular, own = call(
        third_kernel,
        (block, pair),
        particular,
        left_map,
        right_map,
        outside,
        flux,
        goal,
        ratio,
        got,
        scratch=(held,),
    )
    others = [flip_permute(own, flip) for flip in (1, 2, 3)]
    near, message = call(gather_kernel, (pair, pair), own, *others)
    far = [flip_permute(message[min(flip, 2) - 1], flip * GROUP) for flip in (1, 2, 3)]
    return call(
        last_kernel,
        (block, block),
        particular,
        left_map,
        right_map,
        factor,
        got,
        own,
        near,
        *far,
        remote_outs=True,
        scratch=(held, held, pltpu.SemaphoreType.DMA((groups, 2))),
    )


def solution(mesh):
    spec = P("rad", "azi", None)
    return jax.shard_map(
        body, mesh=mesh, in_specs=(spec,) * 5, out_specs=(spec, spec), check_vma=False
    )
```

```python
import jax
import jax.numpy as jnp
from jax import lax
from jax.experimental import pallas as pl
from jax.experimental.pallas import tpu as pltpu
from jax.sharding import PartitionSpec as P

radial_weight = 8.0
azimuth_weight = 0.25
axial_weight = 0.25
flow_weight = 0.5
mass_weight = 1.0
heat_weight = 0.25
arrhenius_exponent = 2.0
slope_weight = 2.0

SUB, LANE = 8, 128
GROUP = 4
PIECE = 16
F32 = jnp.float32


def geometry(rows):
    total = rows * lax.axis_size("rad")
    stiffness = radial_weight * rows * rows
    first = (lax.axis_index("rad") * rows).astype(F32)
    links = [stiffness + (stiffness / total) * (first + float(i)) for i in range(rows + 1)]
    radii = [1.0 + (first + (i + 0.5)) * (1.0 / total) for i in range(rows)]
    return links, radii


def splat(scalar):
    return jnp.full((1, LANE), scalar, F32)


def wide(row, width):
    return jnp.concatenate([row] * (width // LANE), axis=1)


def tiles_of(ref, group, plane, width):
    per = width // LANE
    return jnp.concatenate([ref[group * per + t, plane] for t in range(per)], axis=1)


def put_tiles(ref, group, plane, value):
    per = value.shape[1] // LANE
    for t in range(per):
        ref[group * per + t, plane] = value[:, t * LANE : (t + 1) * LANE]


def lane_next(value):
    width = value.shape[1]
    lane = lax.broadcasted_iota(jnp.int32, value.shape, 1)
    return jnp.where(lane == width - 1, 0.0, pltpu.roll(value, width - 1, 1))


def lane_prev(value):
    lane = lax.broadcasted_iota(jnp.int32, value.shape, 1)
    return jnp.where(lane == 0, 0.0, pltpu.roll(value, 1, 1))


def shunt_of(hot, size, drag_flux, radius, base):
    drag = jnp.exp(-arrhenius_exponent * (hot - 1.0)) * size
    heating = (heat_weight * arrhenius_exponent) * (drag * size)
    return drag, radius * (base + flow_weight * drag_flux + heating)


def ladder(shunts, links, inverse_links):
    rows = len(shunts)
    ratios, lefts = [], []
    through = jnp.full(shunts[0].shape, links[0], F32)
    pivot = shunts[0] + links[0]
    for i in range(rows):
        if i > 0:
            pivot = shunts[i] + ratios[-1] * pivot
        lefts.append(through)
        if i < rows - 1:
            step = links[i + 1] / (links[i + 1] + pivot)
            ratios.append(step)
            through = step * through
    from_left = jnp.zeros_like(through)
    from_right = jnp.ones_like(through)
    left_maps, right_maps = [from_left], [from_right]
    for i in range(rows - 2, -1, -1):
        from_left = ratios[i] * (lefts[i] * inverse_links[i + 1] + from_left)
        from_right = ratios[i] * from_right
        left_maps.append(from_left)
        right_maps.append(from_right)
    inner = links[0] * (1.0 - from_left)
    return ratios, left_maps[::-1], right_maps[::-1], (through, inner, pivot)


def base_shunts(radii):
    out = []
    for radius in radii:
        r = splat(radius)
        out.append(2.0 * azimuth_weight / (r * r) + (mass_weight + 2.0 * axial_weight))
    return out


def matrix_kernel(
    heat,
    deform,
    flux,
    goal,
    ratio,
    left_map,
    right_map,
    factor,
    ahead,
    given,
    condensed,
):
    rows, azimuths, width = heat.shape
    links, radii = geometry(rows)
    inverse_links = [wide(1.0 / splat(link), width) for link in links]
    bases = [wide(base, width) for base in base_shunts(radii)]
    for group in range(azimuths // SUB):
        here = pl.ds(group * SUB, SUB)
        shunts = []
        for i in range(rows):
            hot = heat[i, here, :]
            moving = flux[i, here, :]
            drag, shunt = shunt_of(hot, deform[i, here, :], moving, radii[i], bases[i])
            shunts.append(shunt)
            lane = lax.broadcasted_iota(jnp.int32, hot.shape, 1)
            last = lane == width - 1
            rise = jnp.where(last, 0.0, pltpu.roll(hot, width - 1, 1) - hot)
            ahead[i, here, :] = jnp.where(
                last, 0.0, radii[i] * axial_weight + (radii[i] * flow_weight) * moving
            )
            given[i, here, :] = radii[i] * goal[i, here, :]
            factor[i, here, :] = slope_weight * rise - (2.0 * heat_weight) * drag
        ratios, lefts, rights, ports = ladder(shunts, links, inverse_links)
        for i in range(rows):
            ratio[i, here, :] = ratios[i] if i < rows - 1 else jnp.zeros_like(hot)
            left_map[i, here, :] = lefts[i]
            right_map[i, here, :] = rights[i]
        for plane, port in enumerate(ports):
            put_tiles(condensed, group, plane, port)


def edge_kernel(heat, deform, flux, goal, old, low_edge, high_edge, held, ready):
    rows, azimuths, width = heat.shape
    ends = ((0, 1, low_edge), (azimuths - 1, azimuths - 2, high_edge))
    copies = []
    for e, (at, inner, _) in enumerate(ends):
        for k, (source, line) in enumerate(
            ((heat, at), (deform, at), (flux, at), (goal, at), (old, at), (old, inner))
        ):
            copy = pltpu.make_async_copy(source.at[:, line, :], held.at[e, k], ready.at[e, k])
            copy.start()
            copies.append(copy)
    total = rows * lax.axis_size("rad")
    first = (lax.axis_index("rad") * rows).astype(F32)
    row = lax.broadcasted_iota(jnp.int32, (rows, width), 0).astype(F32)
    radius = 1.0 + (first + (row + 0.5)) * (1.0 / total)
    base = 2.0 * azimuth_weight / (radius * radius) + (mass_weight + 2.0 * axial_weight)
    quarter = azimuth_weight / radius
    for e, (_, _, out) in enumerate(ends):
        for copy in copies[6 * e : 6 * e + 6]:
            copy.wait()
        hot, size, moving, given, centre, beside = [held[e, k] for k in range(6)]
        _, shunt = shunt_of(hot, size, moving, radius, base)
        out[0] = shunt
        out[1] = radius * explicit(centre, moving, given) + quarter * beside
        out[2] = centre


def explicit(centre, moving, given):
    after = lane_next(centre)
    return (
        given
        + axial_weight * (lane_prev(centre) + after)
        + flow_weight * moving * after
        + mass_weight * centre
    )


def place(padded, group, i, value):
    for t in range(value.shape[1] // LANE):
        padded[i, t, pl.ds((group + 1) * SUB, SUB), :] = value[:, t * LANE : (t + 1) * LANE]


def place_row(padded, at, i, value):
    for t in range(value.shape[1] // LANE):
        padded[i, t, at : at + 1, :] = value[:, t * LANE : (t + 1) * LANE]


def sources(group, padded, ahead, given, behind, radii, quarter):
    rows, tiles = padded.shape[:2]
    here = pl.ds(group * SUB, SUB)

    def lines(i, shift):
        at = pl.ds((group + 1) * SUB + shift, SUB)
        return jnp.concatenate([padded[i, t, at, :] for t in range(tiles)], axis=1)

    out = []
    for i in range(rows):
        centre = lines(i, 0)
        width = centre.shape[1]
        value = given[i, here, :] + ahead[i, here, :] * pltpu.roll(centre, width - 1, 1)
        value = value + behind[i] * pltpu.roll(centre, 1, 1)
        value = value + (radii[i] * mass_weight) * centre
        out.append(value + quarter[i] * (lines(i, -1) + lines(i, 1)))
    return out


def substitute(source, ratios, inverse_links):
    rows = len(source)
    currents = [source[0]]
    for i in range(1, rows):
        currents.append(source[i] + ratios[i - 1] * currents[-1])
    value = jnp.zeros_like(source[0])
    values = [value]
    for i in range(rows - 2, -1, -1):
        value = ratios[i] * (currents[i] * inverse_links[i + 1] + value)
        values.append(value)
    return values[::-1], currents[-1]


def local_solve(group, source, ratio, inverse_links, particular):
    rows = len(source)
    here = pl.ds(group * SUB, SUB)
    ratios = [ratio[i, here, :] for i in range(rows - 1)]
    values, outer = substitute(source, ratios, inverse_links)
    for i in range(rows):
        particular[i, here, :] = values[i]
    return values[0], outer


def tables(rows, width):
    links, radii = geometry(rows)
    inverse_links = [wide(1.0 / splat(link), width) for link in links]
    quarter = [wide(azimuth_weight / splat(radius), width) for radius in radii]
    first = lax.broadcasted_iota(jnp.int32, (1, width), 1) == 0
    behind = [jnp.where(first, 0.0, radius * axial_weight) for radius in radii]
    return links, radii, inverse_links, quarter, behind


def first_kernel(old, ahead, given, ratio, particular, ports, padded):
    rows, azimuths, width = old.shape
    links, radii, inverse_links, quarter, behind = tables(rows, width)
    for i in range(rows):
        place_row(padded, SUB - 1, i, jnp.zeros((1, width), F32))
        place_row(padded, SUB + azimuths, i, jnp.zeros((1, width), F32))
        for group in range(azimuths // SUB):
            place(padded, group, i, old[i, pl.ds(group * SUB, SUB), :])
    for group in range(azimuths // SUB):
        source = sources(group, padded, ahead, given, behind, radii, quarter)
        inner, outer = local_solve(group, source, ratio, inverse_links, particular)
        put_tiles(ports, group, 0, links[0] * inner)
        put_tiles(ports, group, 1, outer)


def pair_of(below, above):
    return jnp.concatenate([below, above], axis=0)


def edge_rows(ref, i):
    last = ref.shape[1] - 1
    return pair_of(ref[i, 0:1, :], ref[i, last : last + 1, :])


def join_kernel(old, below, above, ratio, condensed, ports, message, outside):
    rows, azimuths, width = old.shape
    links, radii, inverse_links, quarter, _ = tables(rows, width)
    tiles = message.shape[0]
    per = width // LANE
    message[:, 0:3] = condensed[...]
    message[:, 3:5] = ports[...]
    message[:, 5] = jnp.ones((tiles, SUB, LANE), F32)

    shunts, source, added = [], [], []
    for i in range(rows):
        row = pl.ds(i, 1)
        shunts.append(pair_of(below[0, row, :], above[0, row, :]))
        source.append(pair_of(below[1, row, :], above[1, row, :]) + quarter[i] * edge_rows(old, i))
        added.append(quarter[i] * pair_of(below[2, row, :], above[2, row, :]))
    ratios, lefts, rights, extra = ladder(shunts, links, inverse_links)
    values, outer = substitute(source, ratios, inverse_links)
    changes, change = substitute(added, [edge_rows(ratio, i) for i in range(rows - 1)], inverse_links)
    for i in range(rows):
        for slot, item in enumerate((values, lefts, rights, changes)):
            outside[slot, i] = item[i]
    for e, (at, row) in enumerate(((0, 0), (tiles - per, SUB - 1))):
        for t in range(per):
            lanes = slice(t * LANE, (t + 1) * LANE)
            for plane, port in enumerate((*extra, links[0] * values[0], outer)):
                message[e * per + t, 5, plane : plane + 1, :] = port[e : e + 1, lanes]
            for plane, port in ((3, links[0] * changes[0]), (4, change)):
                message[at + t, plane, row : row + 1, :] = (
                    ports[at + t, plane - 3, row : row + 1, :] + port[e : e + 1, lanes]
                )


def reduced_solve(last_link, through, inner, pivot, left, right):
    segments = len(through)
    inverses, ratios, offsets = [], [], []
    for s in range(segments):
        diagonal = pivot[s] + (inner[s + 1] if s + 1 < segments else last_link)
        given = right[s] + (left[s + 1] if s + 1 < segments else 0.0)
        if s > 0:
            diagonal = diagonal - through[s] * ratios[-1]
            given = given + ratios[-1] * carried
        carried = given
        inverse = 1.0 / diagonal
        inverses.append(inverse)
        offsets.append(given * inverse)
        if s + 1 < segments:
            ratios.append(through[s + 1] * inverse)
    out = []
    for s in range(segments - 1, -1, -1):
        if s + 1 < segments:
            value = offsets[s] + ratios[s] * value
            green = inverses[s] + ratios[s] * ratios[s] * green
            rising = ratios[s] * rising
        else:
            value, green, rising = offsets[s], inverses[s], jnp.ones_like(offsets[s])
        out.append((value, green, rising))
    return out[::-1]


def reduced_kernel(rows, got, sent):
    segments = got.shape[0]
    last_link = 2.0 * radial_weight * rows * rows
    main = reduced_solve(last_link, *[[got[s, p] for s in range(segments)] for p in range(5)])
    extra = reduced_solve(
        last_link, *[[got[s, 5, p : p + 1, :] for s in range(segments)] for p in range(5)]
    )
    zero = jnp.zeros((SUB, LANE), F32)
    for plane in range(3):
        sent[0, 2 * plane] = zero
    for s in range(segments):
        sent[s, 6] = zero
    for s in range(segments):
        value, green, rising = main[s]
        for plane, item in enumerate((value, rising, green / rising)):
            sent[s, 2 * plane + 1] = item
            if s + 1 < segments:
                sent[s + 1, 2 * plane] = item
        sent[s, 6, 1:2, :] = extra[s][0]
        if s + 1 < segments:
            sent[s + 1, 6, 0:1, :] = extra[s][0]


def third_kernel(
    before, left_map, right_map, outside, ahead, given, ratio, got, particular, own, padded
):
    rows, azimuths, width = before.shape
    links, radii, inverse_links, quarter, behind = tables(rows, width)
    per = width // LANE
    groups = azimuths // SUB
    sub = lax.broadcasted_iota(jnp.int32, (SUB, width), 0)

    def beyond(end):
        return pair_of(
            *[
                jnp.concatenate([got[e * per + t, 6, end : end + 1, :] for t in range(per)], axis=1)
                for e in range(2)
            ]
        )

    left, right = beyond(0), beyond(1)
    for i in range(rows):
        halo = outside[0, i] + outside[1, i] * left + outside[2, i] * right
        place_row(padded, SUB - 1, i, halo[0:1, :])
        place_row(padded, SUB + azimuths, i, halo[1:2, :])
    for group in range(groups):
        here = pl.ds(group * SUB, SUB)
        left = tiles_of(got, group, 0, width)
        right = tiles_of(got, group, 1, width)
        for i in range(rows):
            value = before[i, here, :] + left_map[i, here, :] * left + right_map[i, here, :] * right
            if group == 0:
                value = value + jnp.where(sub == 0, outside[3, i, 0:1, :], 0.0)
            if group == groups - 1:
                value = value + jnp.where(sub == SUB - 1, outside[3, i, 1:2, :], 0.0)
            place(padded, group, i, value)
    for group in range(groups):
        here = pl.ds(group * SUB, SUB)
        source = sources(group, padded, ahead, given, behind, radii, quarter)
        inner, outer = local_solve(group, source, ratio, inverse_links, particular)
        inner = links[0] * inner
        own[0, here, :] = (
            tiles_of(got, group, 2, width) * inner + tiles_of(got, group, 3, width) * outer
        )
        own[1, here, :] = (
            tiles_of(got, group, 4, width) * inner + tiles_of(got, group, 5, width) * outer
        )


def gather_kernel(own, first, second, third, near, message):
    mine = lax.rem(lax.axis_index("rad"), GROUP)
    block = lax.div(lax.axis_index("rad"), GROUP)
    for group in range(own.shape[1] // SUB):
        here = pl.ds(group * SUB, SUB)
        upward, downward = own[0, here, :], own[1, here, :]
        lower, upper = jnp.zeros_like(upward), downward
        for flip, other in ((1, first), (2, second), (3, third)):
            up, down = other[0, here, :], other[1, here, :]
            upward = upward + up
            downward = downward + down
            below = (mine ^ flip) < mine
            lower = lower + jnp.where(below, up, 0.0)
            upper = upper + jnp.where(below, 0.0, down)
        near[0, here, :] = lower
        near[1, here, :] = upper
        for slot, flip in ((0, 1), (1, 2)):
            message[slot, here, :] = jnp.where((block ^ flip) > block, upward, downward)


def last_kernel(
    particular,
    left_map,
    right_map,
    factor,
    got,
    own,
    near,
    first,
    second,
    third,
    result,
    sensitivity,
    result_out,
    sensitivity_out,
    done,
):
    rows, azimuths, width = particular.shape
    block = lax.div(lax.axis_index("rad"), GROUP)
    copies = []
    for group in range(azimuths // SUB):
        here = pl.ds(group * SUB, SUB)
        lower, upper = near[0, here, :], near[1, here, :]
        for flip, other in ((1, first), (2, second), (3, third)):
            item = other[here, :]
            below = (block ^ flip) < block
            lower = lower + jnp.where(below, item, 0.0)
            upper = upper + jnp.where(below, 0.0, item)
        left = tiles_of(got, group, 4, width) * lower + tiles_of(got, group, 2, width) * upper
        right = (
            tiles_of(got, group, 5, width) * (lower + own[0, here, :])
            + tiles_of(got, group, 3, width) * (upper - own[1, here, :])
        )
        for i in range(rows):
            value = particular[i, here, :] + left_map[i, here, :] * left + right_map[i, here, :] * right
            result_out[i, here, :] = value
            sensitivity_out[i, here, :] = value * factor[i, here, :]
            if (i + 1) % PIECE:
                continue
            part = pl.ds(i + 1 - PIECE, PIECE)
            for k, (source, target) in enumerate(
                ((result_out, result), (sensitivity_out, sensitivity))
            ):
                copy = pltpu.make_async_copy(
                    source.at[part, here, :], target.at[part, here, :], done.at[group, i // PIECE, k]
                )
                copy.start()
                copies.append(copy)
    for copy in copies:
        copy.wait()


def call(kernel, outs, *args, flops=1_000_000, remote=(), remote_outs=False, scratch=(), room=24):
    moved = sum(4 * a.size for a in args) + sum(4 * o.size for o in outs)
    near, away = pl.BlockSpec(memory_space=pltpu.VMEM), pl.BlockSpec(memory_space=pltpu.HBM)
    return pl.pallas_call(
        kernel,
        out_shape=outs,
        in_specs=[away if k in remote else near for k in range(len(args))],
        out_specs=tuple([away if remote_outs else near] * len(outs)),
        scratch_shapes=list(scratch),
        compiler_params=pltpu.CompilerParams(vmem_limit_bytes=room * 2**20),
        cost_estimate=pl.CostEstimate(flops=flops, bytes_accessed=moved, transcendentals=0),
    )(*args)


def swap_edges(low_edge, high_edge):
    count = lax.axis_size("azi")
    below = lax.ppermute(high_edge, "azi", [(i, (i + 1) % count) for i in range(count)])
    above = lax.ppermute(low_edge, "azi", [((i + 1) % count, i) for i in range(count)])
    return below, above


def flip_permute(value, flip):
    return lax.ppermute(value, "rad", [(i, i ^ flip) for i in range(lax.axis_size("rad"))])


def exchange(value):
    return lax.all_to_all(value, "rad", 0, 0, tiled=True)


def body(heat, deform, flux, goal, start):
    rows, azimuths, width = heat.shape
    segments = lax.axis_size("rad")
    groups = azimuths // SUB
    tiles = azimuths * width // (SUB * LANE)
    block = jax.ShapeDtypeStruct((rows, azimuths, width), F32)
    pair = jax.ShapeDtypeStruct((2, azimuths, width), F32)
    edge = jax.ShapeDtypeStruct((3, rows, width), F32)
    held = pltpu.VMEM((rows, azimuths, width), F32)
    padded = pltpu.VMEM((rows, width // LANE, azimuths + 2 * SUB, LANE), F32)

    def planes(count):
        return jax.ShapeDtypeStruct((tiles, count, SUB, LANE), F32)

    edges = call(
        edge_kernel,
        (edge, edge),
        heat,
        deform,
        flux,
        goal,
        start,
        remote=range(5),
        room=54,
        scratch=(pltpu.VMEM((2, 6, rows, width), F32), pltpu.SemaphoreType.DMA((2, 6))),
    )
    below, above = swap_edges(*edges)
    ratio, left_map, right_map, factor, ahead, given, condensed = call(
        matrix_kernel,
        (block, block, block, block, block, block, planes(3)),
        heat,
        deform,
        flux,
        goal,
        flops=20_000_000,
    )
    particular, ports = call(
        first_kernel, (block, planes(2)), start, ahead, given, ratio, scratch=(padded,)
    )
    message, outside = call(
        join_kernel,
        (planes(6), jax.ShapeDtypeStruct((4, rows, 2, width), F32)),
        start,
        below,
        above,
        ratio,
        condensed,
        ports,
    )
    sent = call(
        lambda got, sent: reduced_kernel(rows, got, sent),
        (jax.ShapeDtypeStruct((segments, 7, SUB, LANE), F32),),
        exchange(message),
    )[0]
    got = exchange(sent)
    particular, own = call(
        third_kernel,
        (block, pair),
        particular,
        left_map,
        right_map,
        outside,
        ahead,
        given,
        ratio,
        got,
        scratch=(padded,),
    )
    others = [flip_permute(own, flip) for flip in (1, 2, 3)]
    near, message = call(gather_kernel, (pair, pair), own, *others)
    far = [flip_permute(message[min(flip, 2) - 1], flip * GROUP) for flip in (1, 2, 3)]
    return call(
        last_kernel,
        (block, block),
        particular,
        left_map,
        right_map,
        factor,
        got,
        own,
        near,
        *far,
        remote_outs=True,
        scratch=(held, held, pltpu.SemaphoreType.DMA((groups, rows // PIECE, 2))),
    )


def solution(mesh):
    spec = P("rad", "azi", None)
    return jax.shard_map(
        body, mesh=mesh, in_specs=(spec,) * 5, out_specs=(spec, spec), check_vma=False
    )
```

```python
import jax
import jax.numpy as jnp
from jax import lax
from jax.experimental import pallas as pl
from jax.experimental.pallas import tpu as pltpu
from jax.sharding import PartitionSpec as P

radial_weight = 8.0
azimuth_weight = 0.25
axial_weight = 0.25
flow_weight = 0.5
mass_weight = 1.0
heat_weight = 0.25
arrhenius_exponent = 2.0
slope_weight = 2.0

SUB, LANE = 8, 128
GROUP = 4
PIECE = 16
F32 = jnp.float32


def geometry(rows):
    total = rows * lax.axis_size("rad")
    stiffness = radial_weight * rows * rows
    first = (lax.axis_index("rad") * rows).astype(F32)
    links = [stiffness + (stiffness / total) * (first + float(i)) for i in range(rows + 1)]
    radii = [1.0 + (first + (i + 0.5)) * (1.0 / total) for i in range(rows)]
    return links, radii


def splat(scalar):
    return jnp.full((1, LANE), scalar, F32)


def wide(row, width):
    return jnp.concatenate([row] * (width // LANE), axis=1)


def tiles_of(ref, group, plane, width):
    per = width // LANE
    return jnp.concatenate([ref[group * per + t, plane] for t in range(per)], axis=1)


def put_tiles(ref, group, plane, value):
    per = value.shape[1] // LANE
    for t in range(per):
        ref[group * per + t, plane] = value[:, t * LANE : (t + 1) * LANE]


def lane_next(value):
    width = value.shape[1]
    lane = lax.broadcasted_iota(jnp.int32, value.shape, 1)
    return jnp.where(lane == width - 1, 0.0, pltpu.roll(value, width - 1, 1))


def lane_prev(value):
    lane = lax.broadcasted_iota(jnp.int32, value.shape, 1)
    return jnp.where(lane == 0, 0.0, pltpu.roll(value, 1, 1))


def shunt_of(hot, size, drag_flux, radius, base):
    drag = jnp.exp(-arrhenius_exponent * (hot - 1.0)) * size
    heating = (heat_weight * arrhenius_exponent) * (drag * size)
    return drag, radius * (base + flow_weight * drag_flux + heating)


def ladder(shunts, links, inverse_links):
    rows = len(shunts)
    ratios, lefts = [], []
    through = jnp.full(shunts[0].shape, links[0], F32)
    pivot = shunts[0] + links[0]
    for i in range(rows):
        if i > 0:
            pivot = shunts[i] + ratios[-1] * pivot
        lefts.append(through)
        if i < rows - 1:
            step = links[i + 1] / (links[i + 1] + pivot)
            ratios.append(step)
            through = step * through
    from_left = jnp.zeros_like(through)
    from_right = jnp.ones_like(through)
    left_maps, right_maps = [from_left], [from_right]
    for i in range(rows - 2, -1, -1):
        from_left = ratios[i] * (lefts[i] * inverse_links[i + 1] + from_left)
        from_right = ratios[i] * from_right
        left_maps.append(from_left)
        right_maps.append(from_right)
    inner = links[0] * (1.0 - from_left)
    return ratios, left_maps[::-1], right_maps[::-1], (through, inner, pivot)


def base_shunts(radii):
    out = []
    for radius in radii:
        r = splat(radius)
        out.append(2.0 * azimuth_weight / (r * r) + (mass_weight + 2.0 * axial_weight))
    return out


def matrix_kernel(
    heat,
    deform,
    flux,
    goal,
    ratio,
    left_map,
    right_map,
    factor,
    ahead,
    given,
    condensed,
):
    rows, azimuths, width = heat.shape
    links, radii = geometry(rows)
    inverse_links = [wide(1.0 / splat(link), width) for link in links]
    bases = [wide(base, width) for base in base_shunts(radii)]
    for group in range(azimuths // SUB):
        here = pl.ds(group * SUB, SUB)
        shunts = []
        for i in range(rows):
            hot = heat[i, here, :]
            moving = flux[i, here, :]
            drag, shunt = shunt_of(hot, deform[i, here, :], moving, radii[i], bases[i])
            shunts.append(shunt)
            lane = lax.broadcasted_iota(jnp.int32, hot.shape, 1)
            last = lane == width - 1
            rise = jnp.where(last, 0.0, pltpu.roll(hot, width - 1, 1) - hot)
            ahead[i, here, :] = jnp.where(
                last, 0.0, radii[i] * axial_weight + (radii[i] * flow_weight) * moving
            )
            given[i, here, :] = radii[i] * goal[i, here, :]
            factor[i, here, :] = slope_weight * rise - (2.0 * heat_weight) * drag
        ratios, lefts, rights, ports = ladder(shunts, links, inverse_links)
        for i in range(rows):
            ratio[i, here, :] = ratios[i] if i < rows - 1 else jnp.zeros_like(hot)
            left_map[i, here, :] = lefts[i]
            right_map[i, here, :] = rights[i]
        for plane, port in enumerate(ports):
            put_tiles(condensed, group, plane, port)


def edge_kernel(heat, deform, flux, goal, old, low_edge, high_edge, held, ready):
    rows, azimuths, width = heat.shape
    ends = ((0, 1, low_edge), (azimuths - 1, azimuths - 2, high_edge))
    copies = []
    for e, (at, inner, _) in enumerate(ends):
        for k, (source, line) in enumerate(
            ((heat, at), (deform, at), (flux, at), (goal, at), (old, at), (old, inner))
        ):
            copy = pltpu.make_async_copy(source.at[:, line, :], held.at[e, k], ready.at[e, k])
            copy.start()
            copies.append(copy)
    total = rows * lax.axis_size("rad")
    first = (lax.axis_index("rad") * rows).astype(F32)
    row = lax.broadcasted_iota(jnp.int32, (rows, width), 0).astype(F32)
    radius = 1.0 + (first + (row + 0.5)) * (1.0 / total)
    base = 2.0 * azimuth_weight / (radius * radius) + (mass_weight + 2.0 * axial_weight)
    quarter = azimuth_weight / radius
    for e, (_, _, out) in enumerate(ends):
        for copy in copies[6 * e : 6 * e + 6]:
            copy.wait()
        hot, size, moving, given, centre, beside = [held[e, k] for k in range(6)]
        _, shunt = shunt_of(hot, size, moving, radius, base)
        out[0] = shunt
        out[1] = radius * explicit(centre, moving, given) + quarter * beside
        out[2] = centre


def explicit(centre, moving, given):
    after = lane_next(centre)
    return (
        given
        + axial_weight * (lane_prev(centre) + after)
        + flow_weight * moving * after
        + mass_weight * centre
    )


def place(padded, group, i, value):
    for t in range(value.shape[1] // LANE):
        padded[i, t, pl.ds((group + 1) * SUB, SUB), :] = value[:, t * LANE : (t + 1) * LANE]


def place_row(padded, at, i, value):
    for t in range(value.shape[1] // LANE):
        padded[i, t, at : at + 1, :] = value[:, t * LANE : (t + 1) * LANE]


def sources(group, padded, ahead, given, behind, radii, quarter):
    rows, tiles = padded.shape[:2]
    here = pl.ds(group * SUB, SUB)

    def lines(i, shift):
        at = pl.ds((group + 1) * SUB + shift, SUB)
        return jnp.concatenate([padded[i, t, at, :] for t in range(tiles)], axis=1)

    out = []
    for i in range(rows):
        centre = lines(i, 0)
        width = centre.shape[1]
        value = given[i, here, :] + ahead[i, here, :] * pltpu.roll(centre, width - 1, 1)
        value = value + behind[i] * pltpu.roll(centre, 1, 1)
        value = value + (radii[i] * mass_weight) * centre
        out.append(value + quarter[i] * (lines(i, -1) + lines(i, 1)))
    return out


def substitute(source, ratios, inverse_links):
    rows = len(source)
    currents = [source[0]]
    for i in range(1, rows):
        currents.append(source[i] + ratios[i - 1] * currents[-1])
    value = jnp.zeros_like(source[0])
    values = [value]
    for i in range(rows - 2, -1, -1):
        value = ratios[i] * (currents[i] * inverse_links[i + 1] + value)
        values.append(value)
    return values[::-1], currents[-1]


def local_solve(group, source, ratio, inverse_links, particular):
    rows = len(source)
    here = pl.ds(group * SUB, SUB)
    ratios = [ratio[i, here, :] for i in range(rows - 1)]
    values, outer = substitute(source, ratios, inverse_links)
    for i in range(rows):
        particular[i, here, :] = values[i]
    return values[0], outer


def tables(rows, width):
    links, radii = geometry(rows)
    inverse_links = [wide(1.0 / splat(link), width) for link in links]
    quarter = [wide(azimuth_weight / splat(radius), width) for radius in radii]
    first = lax.broadcasted_iota(jnp.int32, (1, width), 1) == 0
    behind = [jnp.where(first, 0.0, radius * axial_weight) for radius in radii]
    return links, radii, inverse_links, quarter, behind


def first_kernel(old, ahead, given, ratio, particular, ports, padded):
    rows, azimuths, width = old.shape
    links, radii, inverse_links, quarter, behind = tables(rows, width)
    for i in range(rows):
        place_row(padded, SUB - 1, i, jnp.zeros((1, width), F32))
        place_row(padded, SUB + azimuths, i, jnp.zeros((1, width), F32))
        for group in range(azimuths // SUB):
            place(padded, group, i, old[i, pl.ds(group * SUB, SUB), :])
    for group in range(azimuths // SUB):
        source = sources(group, padded, ahead, given, behind, radii, quarter)
        inner, outer = local_solve(group, source, ratio, inverse_links, particular)
        put_tiles(ports, group, 0, links[0] * inner)
        put_tiles(ports, group, 1, outer)


def pair_of(below, above):
    return jnp.concatenate([below, above], axis=0)


def edge_rows(ref, i):
    last = ref.shape[1] - 1
    return pair_of(ref[i, 0:1, :], ref[i, last : last + 1, :])


def join_kernel(old, below, above, ratio, condensed, ports, message, outside):
    rows, azimuths, width = old.shape
    links, radii, inverse_links, quarter, _ = tables(rows, width)
    tiles = message.shape[0]
    per = width // LANE
    message[:, 0:3] = condensed[...]
    message[:, 3:5] = ports[...]
    message[:, 5] = jnp.ones((tiles, SUB, LANE), F32)

    shunts, source, added = [], [], []
    for i in range(rows):
        row = pl.ds(i, 1)
        shunts.append(pair_of(below[0, row, :], above[0, row, :]))
        source.append(pair_of(below[1, row, :], above[1, row, :]) + quarter[i] * edge_rows(old, i))
        added.append(quarter[i] * pair_of(below[2, row, :], above[2, row, :]))
    ratios, lefts, rights, extra = ladder(shunts, links, inverse_links)
    values, outer = substitute(source, ratios, inverse_links)
    changes, change = substitute(added, [edge_rows(ratio, i) for i in range(rows - 1)], inverse_links)
    for i in range(rows):
        for slot, item in enumerate((values, lefts, rights, changes)):
            outside[slot, i] = item[i]
    for e, (at, row) in enumerate(((0, 0), (tiles - per, SUB - 1))):
        for t in range(per):
            lanes = slice(t * LANE, (t + 1) * LANE)
            for plane, port in enumerate((*extra, links[0] * values[0], outer)):
                message[e * per + t, 5, plane : plane + 1, :] = port[e : e + 1, lanes]
            for plane, port in ((3, links[0] * changes[0]), (4, change)):
                message[at + t, plane, row : row + 1, :] = (
                    ports[at + t, plane - 3, row : row + 1, :] + port[e : e + 1, lanes]
                )


def reduced_solve(last_link, through, inner, pivot, left, right):
    segments = len(through)
    inverses, ratios, offsets = [], [], []
    for s in range(segments):
        diagonal = pivot[s] + (inner[s + 1] if s + 1 < segments else last_link)
        given = right[s] + (left[s + 1] if s + 1 < segments else 0.0)
        if s > 0:
            diagonal = diagonal - through[s] * ratios[-1]
            given = given + ratios[-1] * carried
        carried = given
        inverse = 1.0 / diagonal
        inverses.append(inverse)
        offsets.append(given * inverse)
        if s + 1 < segments:
            ratios.append(through[s + 1] * inverse)
    out = []
    for s in range(segments - 1, -1, -1):
        if s + 1 < segments:
            value = offsets[s] + ratios[s] * value
            green = inverses[s] + ratios[s] * ratios[s] * green
            rising = ratios[s] * rising
        else:
            value, green, rising = offsets[s], inverses[s], jnp.ones_like(offsets[s])
        out.append((value, green, rising))
    return out[::-1]


def reduced_kernel(rows, got, sent):
    segments = got.shape[0]
    last_link = 2.0 * radial_weight * rows * rows
    main = reduced_solve(last_link, *[[got[s, p] for s in range(segments)] for p in range(5)])
    extra = reduced_solve(
        last_link, *[[got[s, 5, p : p + 1, :] for s in range(segments)] for p in range(5)]
    )
    zero = jnp.zeros((SUB, LANE), F32)
    for plane in (0, 2):
        sent[0, plane] = zero
    for s in range(segments):
        sent[s, 5] = zero
    for s in range(segments):
        value, green, rising = main[s]
        sent[s, 1] = value
        sent[s, 3] = rising
        sent[s, 4] = green / rising
        sent[s, 5, 1:2, :] = extra[s][0]
        if s + 1 < segments:
            sent[s + 1, 0] = value
            sent[s + 1, 2] = rising
            sent[s + 1, 5, 0:1, :] = extra[s][0]


def third_kernel(
    before,
    left_map,
    right_map,
    outside,
    ahead,
    given,
    ratio,
    condensed,
    got,
    particular,
    own,
    fall,
    padded,
):
    rows, azimuths, width = before.shape
    links, radii, inverse_links, quarter, behind = tables(rows, width)
    per = width // LANE
    groups = azimuths // SUB
    sub = lax.broadcasted_iota(jnp.int32, (SUB, width), 0)

    def beyond(end):
        return pair_of(
            *[
                jnp.concatenate([got[e * per + t, 5, end : end + 1, :] for t in range(per)], axis=1)
                for e in range(2)
            ]
        )

    left, right = beyond(0), beyond(1)
    for i in range(rows):
        halo = outside[0, i] + outside[1, i] * left + outside[2, i] * right
        place_row(padded, SUB - 1, i, halo[0:1, :])
        place_row(padded, SUB + azimuths, i, halo[1:2, :])
    for group in range(groups):
        here = pl.ds(group * SUB, SUB)
        left = tiles_of(got, group, 0, width)
        right = tiles_of(got, group, 1, width)
        for i in range(rows):
            value = before[i, here, :] + left_map[i, here, :] * left + right_map[i, here, :] * right
            if group == 0:
                value = value + jnp.where(sub == 0, outside[3, i, 0:1, :], 0.0)
            if group == groups - 1:
                value = value + jnp.where(sub == SUB - 1, outside[3, i, 1:2, :], 0.0)
            place(padded, group, i, value)
    for group in range(groups):
        here = pl.ds(group * SUB, SUB)
        source = sources(group, padded, ahead, given, behind, radii, quarter)
        inner, outer = local_solve(group, source, ratio, inverse_links, particular)
        inner = links[0] * inner
        rise_left, rise_right, fall_right = [tiles_of(got, group, plane, width) for plane in (2, 3, 4)]
        through = tiles_of(condensed, group, 0, width)
        fall_left = (1.0 / through + rise_left * fall_right) / rise_right
        fall_left = jnp.where(lax.axis_index("rad") == 0, 0.0, fall_left)
        fall[here, :] = fall_left
        own[0, here, :] = rise_left * inner + rise_right * outer
        own[1, here, :] = fall_left * inner + fall_right * outer


def gather_kernel(own, first, second, third, near, message):
    mine = lax.rem(lax.axis_index("rad"), GROUP)
    block = lax.div(lax.axis_index("rad"), GROUP)
    for group in range(own.shape[1] // SUB):
        here = pl.ds(group * SUB, SUB)
        upward, downward = own[0, here, :], own[1, here, :]
        lower, upper = jnp.zeros_like(upward), downward
        for flip, other in ((1, first), (2, second), (3, third)):
            up, down = other[0, here, :], other[1, here, :]
            upward = upward + up
            downward = downward + down
            below = (mine ^ flip) < mine
            lower = lower + jnp.where(below, up, 0.0)
            upper = upper + jnp.where(below, 0.0, down)
        near[0, here, :] = lower
        near[1, here, :] = upper
        for slot, flip in ((0, 1), (1, 2)):
            message[slot, here, :] = jnp.where((block ^ flip) > block, upward, downward)


def last_kernel(
    particular,
    left_map,
    right_map,
    factor,
    got,
    own,
    fall,
    near,
    first,
    second,
    third,
    result,
    sensitivity,
    result_out,
    sensitivity_out,
    done,
):
    rows, azimuths, width = particular.shape
    block = lax.div(lax.axis_index("rad"), GROUP)
    copies = []
    for group in range(azimuths // SUB):
        here = pl.ds(group * SUB, SUB)
        lower, upper = near[0, here, :], near[1, here, :]
        for flip, other in ((1, first), (2, second), (3, third)):
            item = other[here, :]
            below = (block ^ flip) < block
            lower = lower + jnp.where(below, item, 0.0)
            upper = upper + jnp.where(below, 0.0, item)
        left = fall[here, :] * lower + tiles_of(got, group, 2, width) * upper
        right = (
            tiles_of(got, group, 4, width) * (lower + own[0, here, :])
            + tiles_of(got, group, 3, width) * (upper - own[1, here, :])
        )
        for i in range(rows):
            value = particular[i, here, :] + left_map[i, here, :] * left + right_map[i, here, :] * right
            result_out[i, here, :] = value
            sensitivity_out[i, here, :] = value * factor[i, here, :]
            if (i + 1) % PIECE:
                continue
            part = pl.ds(i + 1 - PIECE, PIECE)
            for k, (source, target) in enumerate(
                ((result_out, result), (sensitivity_out, sensitivity))
            ):
                copy = pltpu.make_async_copy(
                    source.at[part, here, :], target.at[part, here, :], done.at[group, i // PIECE, k]
                )
                copy.start()
                copies.append(copy)
    for copy in copies:
        copy.wait()


def call(kernel, outs, *args, flops=1_000_000, remote=(), remote_outs=False, scratch=(), room=24):
    moved = sum(4 * a.size for a in args) + sum(4 * o.size for o in outs)
    near, away = pl.BlockSpec(memory_space=pltpu.VMEM), pl.BlockSpec(memory_space=pltpu.HBM)
    return pl.pallas_call(
        kernel,
        out_shape=outs,
        in_specs=[away if k in remote else near for k in range(len(args))],
        out_specs=tuple([away if remote_outs else near] * len(outs)),
        scratch_shapes=list(scratch),
        compiler_params=pltpu.CompilerParams(vmem_limit_bytes=room * 2**20),
        cost_estimate=pl.CostEstimate(flops=flops, bytes_accessed=moved, transcendentals=0),
    )(*args)


def swap_edges(low_edge, high_edge):
    count = lax.axis_size("azi")
    below = lax.ppermute(high_edge, "azi", [(i, (i + 1) % count) for i in range(count)])
    above = lax.ppermute(low_edge, "azi", [((i + 1) % count, i) for i in range(count)])
    return below, above


def flip_permute(value, flip):
    return lax.ppermute(value, "rad", [(i, i ^ flip) for i in range(lax.axis_size("rad"))])


def exchange(value):
    return lax.all_to_all(value, "rad", 0, 0, tiled=True)


def body(heat, deform, flux, goal, start):
    rows, azimuths, width = heat.shape
    segments = lax.axis_size("rad")
    groups = azimuths // SUB
    tiles = azimuths * width // (SUB * LANE)
    block = jax.ShapeDtypeStruct((rows, azimuths, width), F32)
    pair = jax.ShapeDtypeStruct((2, azimuths, width), F32)
    edge = jax.ShapeDtypeStruct((3, rows, width), F32)
    held = pltpu.VMEM((rows, azimuths, width), F32)
    padded = pltpu.VMEM((rows, width // LANE, azimuths + 2 * SUB, LANE), F32)

    def planes(count):
        return jax.ShapeDtypeStruct((tiles, count, SUB, LANE), F32)

    edges = call(
        edge_kernel,
        (edge, edge),
        heat,
        deform,
        flux,
        goal,
        start,
        remote=range(5),
        room=54,
        scratch=(pltpu.VMEM((2, 6, rows, width), F32), pltpu.SemaphoreType.DMA((2, 6))),
    )
    below, above = swap_edges(*edges)
    ratio, left_map, right_map, factor, ahead, given, condensed = call(
        matrix_kernel,
        (block, block, block, block, block, block, planes(3)),
        heat,
        deform,
        flux,
        goal,
        flops=20_000_000,
    )
    particular, ports = call(
        first_kernel, (block, planes(2)), start, ahead, given, ratio, scratch=(padded,)
    )
    message, outside = call(
        join_kernel,
        (planes(6), jax.ShapeDtypeStruct((4, rows, 2, width), F32)),
        start,
        below,
        above,
        ratio,
        condensed,
        ports,
    )
    sent = call(
        lambda got, sent: reduced_kernel(rows, got, sent),
        (jax.ShapeDtypeStruct((segments, 6, SUB, LANE), F32),),
        exchange(message),
    )[0]
    got = exchange(sent)
    particular, own, fall = call(
        third_kernel,
        (block, pair, jax.ShapeDtypeStruct((azimuths, width), F32)),
        particular,
        left_map,
        right_map,
        outside,
        ahead,
        given,
        ratio,
        condensed,
        got,
        scratch=(padded,),
    )
    others = [flip_permute(own, flip) for flip in (1, 2, 3)]
    near, message = call(gather_kernel, (pair, pair), own, *others)
    far = [flip_permute(message[min(flip, 2) - 1], flip * GROUP) for flip in (1, 2, 3)]
    return call(
        last_kernel,
        (block, block),
        particular,
        left_map,
        right_map,
        factor,
        got,
        own,
        fall,
        near,
        *far,
        remote_outs=True,
        scratch=(held, held, pltpu.SemaphoreType.DMA((groups, rows // PIECE, 2))),
    )


def solution(mesh):
    spec = P("rad", "azi", None)
    return jax.shard_map(
        body, mesh=mesh, in_specs=(spec,) * 5, out_specs=(spec, spec), check_vma=False
    )
```

```python
import jax
import jax.numpy as jnp
from jax import lax
from jax.experimental import pallas as pl
from jax.experimental.pallas import tpu as pltpu
from jax.sharding import PartitionSpec as P

radial_weight = 8.0
azimuth_weight = 0.25
axial_weight = 0.25
flow_weight = 0.5
mass_weight = 1.0
heat_weight = 0.25
arrhenius_exponent = 2.0
slope_weight = 2.0

SUB, LANE = 8, 128
GROUP = 4
PIECE = 16
F32 = jnp.float32


def geometry(rows):
    total = rows * lax.axis_size("rad")
    stiffness = radial_weight * rows * rows
    first = (lax.axis_index("rad") * rows).astype(F32)
    links = [stiffness + (stiffness / total) * (first + float(i)) for i in range(rows + 1)]
    radii = [1.0 + (first + (i + 0.5)) * (1.0 / total) for i in range(rows)]
    return links, radii


def splat(scalar):
    return jnp.full((1, LANE), scalar, F32)


def wide(row, width):
    return jnp.concatenate([row] * (width // LANE), axis=1)


def tiles_of(ref, group, plane, width):
    per = width // LANE
    return jnp.concatenate([ref[group * per + t, plane] for t in range(per)], axis=1)


def put_tiles(ref, group, plane, value):
    per = value.shape[1] // LANE
    for t in range(per):
        ref[group * per + t, plane] = value[:, t * LANE : (t + 1) * LANE]


def lane_next(value):
    width = value.shape[1]
    lane = lax.broadcasted_iota(jnp.int32, value.shape, 1)
    return jnp.where(lane == width - 1, 0.0, pltpu.roll(value, width - 1, 1))


def lane_prev(value):
    lane = lax.broadcasted_iota(jnp.int32, value.shape, 1)
    return jnp.where(lane == 0, 0.0, pltpu.roll(value, 1, 1))


def shunt_of(hot, size, drag_flux, radius, base):
    drag = jnp.exp(-arrhenius_exponent * (hot - 1.0)) * size
    heating = (heat_weight * arrhenius_exponent) * (drag * size)
    return drag, radius * (base + flow_weight * drag_flux + heating)


def ladder(shunts, links, inverse_links):
    rows = len(shunts)
    ratios, lefts = [], []
    through = jnp.full(shunts[0].shape, links[0], F32)
    pivot = shunts[0] + links[0]
    for i in range(rows):
        if i > 0:
            pivot = shunts[i] + ratios[-1] * pivot
        lefts.append(through)
        if i < rows - 1:
            step = links[i + 1] / (links[i + 1] + pivot)
            ratios.append(step)
            through = step * through
    from_left = jnp.zeros_like(through)
    from_right = jnp.ones_like(through)
    left_maps, right_maps = [from_left], [from_right]
    for i in range(rows - 2, -1, -1):
        from_left = ratios[i] * (lefts[i] * inverse_links[i + 1] + from_left)
        from_right = ratios[i] * from_right
        left_maps.append(from_left)
        right_maps.append(from_right)
    inner = links[0] * (1.0 - from_left)
    return ratios, left_maps[::-1], right_maps[::-1], (through, inner, pivot)


def base_shunts(radii):
    out = []
    for radius in radii:
        r = splat(radius)
        out.append(2.0 * azimuth_weight / (r * r) + (mass_weight + 2.0 * axial_weight))
    return out


def matrix_kernel(
    heat,
    deform,
    flux,
    goal,
    ratio,
    left_map,
    right_map,
    factor,
    ahead,
    given,
    condensed,
):
    rows, azimuths, width = heat.shape
    links, radii = geometry(rows)
    inverse_links = [wide(1.0 / splat(link), width) for link in links]
    bases = [wide(base, width) for base in base_shunts(radii)]
    for group in range(azimuths // SUB):
        here = pl.ds(group * SUB, SUB)
        shunts = []
        for i in range(rows):
            hot = heat[i, here, :]
            moving = flux[i, here, :]
            drag, shunt = shunt_of(hot, deform[i, here, :], moving, radii[i], bases[i])
            shunts.append(shunt)
            lane = lax.broadcasted_iota(jnp.int32, hot.shape, 1)
            last = lane == width - 1
            rise = jnp.where(last, 0.0, pltpu.roll(hot, width - 1, 1) - hot)
            ahead[i, here, :] = jnp.where(
                last, 0.0, radii[i] * axial_weight + (radii[i] * flow_weight) * moving
            )
            given[i, here, :] = radii[i] * goal[i, here, :]
            factor[i, here, :] = slope_weight * rise - (2.0 * heat_weight) * drag
        ratios, lefts, rights, ports = ladder(shunts, links, inverse_links)
        for i in range(rows):
            ratio[i, here, :] = ratios[i] if i < rows - 1 else jnp.zeros_like(hot)
            left_map[i, here, :] = lefts[i]
            right_map[i, here, :] = rights[i]
        for plane, port in enumerate(ports):
            put_tiles(condensed, group, plane, port)


def edge_kernel(heat, deform, flux, goal, old, low_edge, high_edge, held, ready):
    rows, azimuths, width = heat.shape
    ends = ((0, 1, low_edge), (azimuths - 1, azimuths - 2, high_edge))
    copies = []
    for e, (at, inner, _) in enumerate(ends):
        for k, (source, line) in enumerate(
            ((heat, at), (deform, at), (flux, at), (goal, at), (old, at), (old, inner))
        ):
            copy = pltpu.make_async_copy(source.at[:, line, :], held.at[e, k], ready.at[e, k])
            copy.start()
            copies.append(copy)
    total = rows * lax.axis_size("rad")
    first = (lax.axis_index("rad") * rows).astype(F32)
    row = lax.broadcasted_iota(jnp.int32, (rows, width), 0).astype(F32)
    radius = 1.0 + (first + (row + 0.5)) * (1.0 / total)
    base = 2.0 * azimuth_weight / (radius * radius) + (mass_weight + 2.0 * axial_weight)
    quarter = azimuth_weight / radius
    for e, (_, _, out) in enumerate(ends):
        for copy in copies[6 * e : 6 * e + 6]:
            copy.wait()
        hot, size, moving, given, centre, beside = [held[e, k] for k in range(6)]
        _, shunt = shunt_of(hot, size, moving, radius, base)
        out[0] = shunt
        out[1] = radius * explicit(centre, moving, given) + quarter * beside
        out[2] = centre


def explicit(centre, moving, given):
    after = lane_next(centre)
    return (
        given
        + axial_weight * (lane_prev(centre) + after)
        + flow_weight * moving * after
        + mass_weight * centre
    )


def place(padded, group, i, value):
    for t in range(value.shape[1] // LANE):
        padded[i, t, pl.ds((group + 1) * SUB, SUB), :] = value[:, t * LANE : (t + 1) * LANE]


def place_row(padded, at, i, value):
    for t in range(value.shape[1] // LANE):
        padded[i, t, at : at + 1, :] = value[:, t * LANE : (t + 1) * LANE]


def sources(group, padded, ahead, given, behind, radii, quarter):
    rows, tiles = padded.shape[:2]
    here = pl.ds(group * SUB, SUB)

    def lines(i, shift):
        at = pl.ds((group + 1) * SUB + shift, SUB)
        return jnp.concatenate([padded[i, t, at, :] for t in range(tiles)], axis=1)

    out = []
    for i in range(rows):
        centre = lines(i, 0)
        width = centre.shape[1]
        value = given[i, here, :] + ahead[i, here, :] * pltpu.roll(centre, width - 1, 1)
        value = value + behind[i] * pltpu.roll(centre, 1, 1)
        value = value + (radii[i] * mass_weight) * centre
        out.append(value + quarter[i] * (lines(i, -1) + lines(i, 1)))
    return out


def substitute(source, ratios, inverse_links):
    rows = len(source)
    currents = [source[0]]
    for i in range(1, rows):
        currents.append(source[i] + ratios[i - 1] * currents[-1])
    value = jnp.zeros_like(source[0])
    values = [value]
    for i in range(rows - 2, -1, -1):
        value = ratios[i] * (currents[i] * inverse_links[i + 1] + value)
        values.append(value)
    return values[::-1], currents[-1]


def local_solve(group, source, ratio, inverse_links, particular):
    rows = len(source)
    here = pl.ds(group * SUB, SUB)
    ratios = [ratio[i, here, :] for i in range(rows - 1)]
    values, outer = substitute(source, ratios, inverse_links)
    for i in range(rows):
        particular[i, here, :] = values[i]
    return values[0], outer


def tables(rows, width):
    links, radii = geometry(rows)
    inverse_links = [wide(1.0 / splat(link), width) for link in links]
    quarter = [wide(azimuth_weight / splat(radius), width) for radius in radii]
    first = lax.broadcasted_iota(jnp.int32, (1, width), 1) == 0
    behind = [jnp.where(first, 0.0, radius * axial_weight) for radius in radii]
    return links, radii, inverse_links, quarter, behind


def first_kernel(old, ahead, given, ratio, particular, ports, padded):
    rows, azimuths, width = old.shape
    links, radii, inverse_links, quarter, behind = tables(rows, width)
    for i in range(rows):
        place_row(padded, SUB - 1, i, jnp.zeros((1, width), F32))
        place_row(padded, SUB + azimuths, i, jnp.zeros((1, width), F32))
        for group in range(azimuths // SUB):
            place(padded, group, i, old[i, pl.ds(group * SUB, SUB), :])
    for group in range(azimuths // SUB):
        source = sources(group, padded, ahead, given, behind, radii, quarter)
        inner, outer = local_solve(group, source, ratio, inverse_links, particular)
        put_tiles(ports, group, 0, links[0] * inner)
        put_tiles(ports, group, 1, outer)


def pair_of(below, above):
    return jnp.concatenate([below, above], axis=0)


def edge_rows(ref, i):
    last = ref.shape[1] - 1
    return pair_of(ref[i, 0:1, :], ref[i, last : last + 1, :])


def join_kernel(old, below, above, ratio, condensed, ports, message, outside):
    rows, azimuths, width = old.shape
    links, radii, inverse_links, quarter, _ = tables(rows, width)
    tiles = message.shape[0]
    per = width // LANE
    message[:, 0:3] = condensed[...]
    message[:, 3:5] = ports[...]
    message[:, 5] = jnp.ones((tiles, SUB, LANE), F32)

    shunts, source, added = [], [], []
    for i in range(rows):
        row = pl.ds(i, 1)
        shunts.append(pair_of(below[0, row, :], above[0, row, :]))
        source.append(pair_of(below[1, row, :], above[1, row, :]) + quarter[i] * edge_rows(old, i))
        added.append(quarter[i] * pair_of(below[2, row, :], above[2, row, :]))
    ratios, lefts, rights, extra = ladder(shunts, links, inverse_links)
    values, outer = substitute(source, ratios, inverse_links)
    changes, change = substitute(added, [edge_rows(ratio, i) for i in range(rows - 1)], inverse_links)
    for i in range(rows):
        for slot, item in enumerate((values, lefts, rights, changes)):
            outside[slot, i] = item[i]
    for e, (at, row) in enumerate(((0, 0), (tiles - per, SUB - 1))):
        for t in range(per):
            lanes = slice(t * LANE, (t + 1) * LANE)
            for plane, port in enumerate((*extra, links[0] * values[0], outer)):
                message[e * per + t, 5, plane : plane + 1, :] = port[e : e + 1, lanes]
            for plane, port in ((3, links[0] * changes[0]), (4, change)):
                message[at + t, plane, row : row + 1, :] = (
                    ports[at + t, plane - 3, row : row + 1, :] + port[e : e + 1, lanes]
                )


def reduced_solve(last_link, through, inner, pivot, left, right):
    segments = len(through)
    inverses, ratios, offsets = [], [], []
    for s in range(segments):
        diagonal = pivot[s] + (inner[s + 1] if s + 1 < segments else last_link)
        given = right[s] + (left[s + 1] if s + 1 < segments else 0.0)
        if s > 0:
            diagonal = diagonal - through[s] * ratios[-1]
            given = given + ratios[-1] * carried
        carried = given
        inverse = 1.0 / diagonal
        inverses.append(inverse)
        offsets.append(given * inverse)
        if s + 1 < segments:
            ratios.append(through[s + 1] * inverse)
    out = []
    for s in range(segments - 1, -1, -1):
        if s + 1 < segments:
            value = offsets[s] + ratios[s] * value
            green = inverses[s] + ratios[s] * ratios[s] * green
            rising = ratios[s] * rising
        else:
            value, green, rising = offsets[s], inverses[s], jnp.ones_like(offsets[s])
        out.append((value, green, rising))
    return out[::-1]


def reduced_kernel(rows, got, sent):
    segments = got.shape[0]
    last_link = 2.0 * radial_weight * rows * rows
    main = reduced_solve(last_link, *[[got[s, p] for s in range(segments)] for p in range(5)])
    extra = reduced_solve(
        last_link, *[[got[s, 5, p : p + 1, :] for s in range(segments)] for p in range(5)]
    )
    zero = jnp.zeros((SUB, LANE), F32)
    for plane in (0, 2):
        sent[0, plane] = zero
    for s in range(segments):
        sent[s, 5] = zero
    for s in range(segments):
        value, green, rising = main[s]
        sent[s, 1] = value
        sent[s, 3] = rising
        sent[s, 4] = green / rising
        sent[s, 5, 1:2, :] = extra[s][0]
        if s + 1 < segments:
            sent[s + 1, 0] = value
            sent[s + 1, 2] = rising
            sent[s + 1, 5, 0:1, :] = extra[s][0]


def third_kernel(
    before,
    left_map,
    right_map,
    outside,
    ahead,
    given,
    ratio,
    condensed,
    got,
    particular,
    own,
    fall,
    padded,
):
    rows, azimuths, width = before.shape
    links, radii, inverse_links, quarter, behind = tables(rows, width)
    per = width // LANE
    groups = azimuths // SUB
    sub = lax.broadcasted_iota(jnp.int32, (SUB, width), 0)

    def beyond(end):
        return pair_of(
            *[
                jnp.concatenate([got[e * per + t, 5, end : end + 1, :] for t in range(per)], axis=1)
                for e in range(2)
            ]
        )

    left, right = beyond(0), beyond(1)
    for i in range(rows):
        halo = outside[0, i] + outside[1, i] * left + outside[2, i] * right
        place_row(padded, SUB - 1, i, halo[0:1, :])
        place_row(padded, SUB + azimuths, i, halo[1:2, :])
    for group in range(groups):
        here = pl.ds(group * SUB, SUB)
        left = tiles_of(got, group, 0, width)
        right = tiles_of(got, group, 1, width)
        for i in range(rows):
            value = before[i, here, :] + left_map[i, here, :] * left + right_map[i, here, :] * right
            if group == 0:
                value = value + jnp.where(sub == 0, outside[3, i, 0:1, :], 0.0)
            if group == groups - 1:
                value = value + jnp.where(sub == SUB - 1, outside[3, i, 1:2, :], 0.0)
            place(padded, group, i, value)
    for group in range(groups):
        here = pl.ds(group * SUB, SUB)
        source = sources(group, padded, ahead, given, behind, radii, quarter)
        inner, outer = local_solve(group, source, ratio, inverse_links, particular)
        inner = links[0] * inner
        rise_left, rise_right, fall_right = [tiles_of(got, group, plane, width) for plane in (2, 3, 4)]
        through = tiles_of(condensed, group, 0, width)
        fall_left = (1.0 / through + rise_left * fall_right) / rise_right
        fall_left = jnp.where(lax.axis_index("rad") == 0, 0.0, fall_left)
        fall[here, :] = fall_left
        own[0, here, :] = rise_left * inner + rise_right * outer
        own[1, here, :] = fall_left * inner + fall_right * outer


def gather_kernel(own, first, second, third, near, message):
    mine = lax.rem(lax.axis_index("rad"), GROUP)
    block = lax.div(lax.axis_index("rad"), GROUP)
    for group in range(own.shape[1] // SUB):
        here = pl.ds(group * SUB, SUB)
        upward, downward = own[0, here, :], own[1, here, :]
        lower, upper = jnp.zeros_like(upward), downward
        for flip, other in ((1, first), (2, second), (3, third)):
            up, down = other[0, here, :], other[1, here, :]
            upward = upward + up
            downward = downward + down
            below = (mine ^ flip) < mine
            lower = lower + jnp.where(below, up, 0.0)
            upper = upper + jnp.where(below, 0.0, down)
        near[0, here, :] = lower
        near[1, here, :] = upper
        for slot, flip in ((0, 1), (1, 2)):
            message[slot, here, :] = jnp.where((block ^ flip) > block, upward, downward)


def last_kernel(
    particular,
    left_map,
    right_map,
    factor,
    got,
    own,
    fall,
    near,
    first,
    second,
    third,
    result,
    sensitivity,
    result_out,
    sensitivity_out,
    done,
):
    rows, azimuths, width = particular.shape
    block = lax.div(lax.axis_index("rad"), GROUP)
    copies = []
    for group in range(azimuths // SUB):
        here = pl.ds(group * SUB, SUB)
        lower, upper = near[0, here, :], near[1, here, :]
        for flip, other in ((1, first), (2, second), (3, third)):
            item = other[here, :]
            below = (block ^ flip) < block
            lower = lower + jnp.where(below, item, 0.0)
            upper = upper + jnp.where(below, 0.0, item)
        left = fall[here, :] * lower + tiles_of(got, group, 2, width) * upper
        right = (
            tiles_of(got, group, 4, width) * (lower + own[0, here, :])
            + tiles_of(got, group, 3, width) * (upper - own[1, here, :])
        )
        for i in range(rows):
            value = particular[i, here, :] + left_map[i, here, :] * left + right_map[i, here, :] * right
            result_out[i, here, :] = value
            sensitivity_out[i, here, :] = value * factor[i, here, :]
            if (i + 1) % PIECE:
                continue
            part = pl.ds(i + 1 - PIECE, PIECE)
            for k, (source, target) in enumerate(
                ((result_out, result), (sensitivity_out, sensitivity))
            ):
                copy = pltpu.make_async_copy(
                    source.at[part, here, :], target.at[part, here, :], done.at[group, i // PIECE, k]
                )
                copy.start()
                copies.append(copy)
    for copy in copies:
        copy.wait()


def call(kernel, outs, *args, flops=1_000_000, remote=(), remote_outs=False, scratch=(), room=24):
    moved = sum(4 * a.size for a in args) + sum(4 * o.size for o in outs)
    near, away = pl.BlockSpec(memory_space=pltpu.VMEM), pl.BlockSpec(memory_space=pltpu.HBM)
    return pl.pallas_call(
        kernel,
        out_shape=outs,
        in_specs=[away if k in remote else near for k in range(len(args))],
        out_specs=tuple([away if remote_outs else near] * len(outs)),
        scratch_shapes=list(scratch),
        compiler_params=pltpu.CompilerParams(vmem_limit_bytes=int(room * 2**20)),
        cost_estimate=pl.CostEstimate(flops=flops, bytes_accessed=moved, transcendentals=0),
    )(*args)


def swap_edges(low_edge, high_edge):
    count = lax.axis_size("azi")
    below = lax.ppermute(high_edge, "azi", [(i, (i + 1) % count) for i in range(count)])
    above = lax.ppermute(low_edge, "azi", [((i + 1) % count, i) for i in range(count)])
    return below, above


def flip_permute(value, flip):
    return lax.ppermute(value, "rad", [(i, i ^ flip) for i in range(lax.axis_size("rad"))])


def exchange(value):
    return lax.all_to_all(value, "rad", 0, 0, tiled=True)


def body(heat, deform, flux, goal, start):
    rows, azimuths, width = heat.shape
    segments = lax.axis_size("rad")
    groups = azimuths // SUB
    tiles = azimuths * width // (SUB * LANE)
    block = jax.ShapeDtypeStruct((rows, azimuths, width), F32)
    pair = jax.ShapeDtypeStruct((2, azimuths, width), F32)
    edge = jax.ShapeDtypeStruct((3, rows, width), F32)
    held = pltpu.VMEM((rows, azimuths, width), F32)
    padded = pltpu.VMEM((rows, width // LANE, azimuths + 2 * SUB, LANE), F32)

    def planes(count):
        return jax.ShapeDtypeStruct((tiles, count, SUB, LANE), F32)

    edges = call(
        edge_kernel,
        (edge, edge),
        heat,
        deform,
        flux,
        goal,
        start,
        remote=range(5),
        room=53,
        scratch=(pltpu.VMEM((2, 6, rows, width), F32), pltpu.SemaphoreType.DMA((2, 6))),
    )
    below, above = swap_edges(*edges)
    ratio, left_map, right_map, factor, ahead, given, condensed = call(
        matrix_kernel,
        (block, block, block, block, block, block, planes(3)),
        heat,
        deform,
        flux,
        goal,
        flops=20_000_000,
    )
    particular, ports = call(
        first_kernel, (block, planes(2)), start, ahead, given, ratio, scratch=(padded,)
    )
    message, outside = call(
        join_kernel,
        (planes(6), jax.ShapeDtypeStruct((4, rows, 2, width), F32)),
        start,
        below,
        above,
        ratio,
        condensed,
        ports,
    )
    sent = call(
        lambda got, sent: reduced_kernel(rows, got, sent),
        (jax.ShapeDtypeStruct((segments, 6, SUB, LANE), F32),),
        exchange(message),
    )[0]
    got = exchange(sent)
    particular, own, fall = call(
        third_kernel,
        (block, pair, jax.ShapeDtypeStruct((azimuths, width), F32)),
        particular,
        left_map,
        right_map,
        outside,
        ahead,
        given,
        ratio,
        condensed,
        got,
        scratch=(padded,),
    )
    others = [flip_permute(own, flip) for flip in (1, 2, 3)]
    near, message = call(gather_kernel, (pair, pair), own, *others)
    far = [flip_permute(message[min(flip, 2) - 1], flip * GROUP) for flip in (1, 2, 3)]
    return call(
        last_kernel,
        (block, block),
        particular,
        left_map,
        right_map,
        factor,
        got,
        own,
        fall,
        near,
        *far,
        remote_outs=True,
        scratch=(held, held, pltpu.SemaphoreType.DMA((groups, rows // PIECE, 2))),
    )


def solution(mesh):
    spec = P("rad", "azi", None)
    return jax.shard_map(
        body, mesh=mesh, in_specs=(spec,) * 5, out_specs=(spec, spec), check_vma=False
    )
```

```python
import jax
import jax.numpy as jnp
from jax import lax
from jax.experimental import pallas as pl
from jax.experimental.pallas import tpu as pltpu
from jax.sharding import PartitionSpec as P

radial_weight = 8.0
azimuth_weight = 0.25
axial_weight = 0.25
flow_weight = 0.5
mass_weight = 1.0
heat_weight = 0.25
arrhenius_exponent = 2.0
slope_weight = 2.0

SUB, LANE = 8, 128
GROUP = 4
F32 = jnp.float32


def geometry(rows):
    total = rows * lax.axis_size("rad")
    stiffness = radial_weight * rows * rows
    first = (lax.axis_index("rad") * rows).astype(F32)
    links = [stiffness + (stiffness / total) * (first + float(i)) for i in range(rows + 1)]
    radii = [1.0 + (first + (i + 0.5)) * (1.0 / total) for i in range(rows)]
    return links, radii


def splat(scalar):
    return jnp.full((1, LANE), scalar, F32)


def wide(row, width):
    return jnp.concatenate([row] * (width // LANE), axis=1)


def tiles_of(ref, group, plane, width):
    per = width // LANE
    return jnp.concatenate([ref[group * per + t, plane] for t in range(per)], axis=1)


def put_tiles(ref, group, plane, value):
    per = value.shape[1] // LANE
    for t in range(per):
        ref[group * per + t, plane] = value[:, t * LANE : (t + 1) * LANE]


def lane_next(value):
    width = value.shape[1]
    lane = lax.broadcasted_iota(jnp.int32, value.shape, 1)
    return jnp.where(lane == width - 1, 0.0, pltpu.roll(value, width - 1, 1))


def lane_prev(value):
    lane = lax.broadcasted_iota(jnp.int32, value.shape, 1)
    return jnp.where(lane == 0, 0.0, pltpu.roll(value, 1, 1))


def shunt_of(hot, size, drag_flux, radius, base):
    drag = jnp.exp(-arrhenius_exponent * (hot - 1.0)) * size
    heating = (heat_weight * arrhenius_exponent) * (drag * size)
    return drag, radius * (base + flow_weight * drag_flux + heating)


def ladder(shunts, links, inverse_links):
    rows = len(shunts)
    ratios, lefts = [], []
    through = jnp.full(shunts[0].shape, links[0], F32)
    pivot = shunts[0] + links[0]
    for i in range(rows):
        if i > 0:
            pivot = shunts[i] + ratios[-1] * pivot
        lefts.append(through)
        if i < rows - 1:
            step = links[i + 1] / (links[i + 1] + pivot)
            ratios.append(step)
            through = step * through
    from_left = jnp.zeros_like(through)
    from_right = jnp.ones_like(through)
    left_maps, right_maps = [from_left], [from_right]
    for i in range(rows - 2, -1, -1):
        from_left = ratios[i] * (lefts[i] * inverse_links[i + 1] + from_left)
        from_right = ratios[i] * from_right
        left_maps.append(from_left)
        right_maps.append(from_right)
    inner = links[0] * (1.0 - from_left)
    return ratios, left_maps[::-1], right_maps[::-1], (through, inner, pivot)


def base_shunts(radii):
    out = []
    for radius in radii:
        r = splat(radius)
        out.append(2.0 * azimuth_weight / (r * r) + (mass_weight + 2.0 * axial_weight))
    return out


def matrix_kernel(
    heat,
    deform,
    flux,
    goal,
    ratio,
    left_map,
    right_map,
    factor,
    ahead,
    given,
    condensed,
):
    rows, azimuths, width = heat.shape
    links, radii = geometry(rows)
    inverse_links = [wide(1.0 / splat(link), width) for link in links]
    bases = [wide(base, width) for base in base_shunts(radii)]
    for group in range(azimuths // SUB):
        here = pl.ds(group * SUB, SUB)
        shunts = []
        for i in range(rows):
            hot = heat[i, here, :]
            moving = flux[i, here, :]
            drag, shunt = shunt_of(hot, deform[i, here, :], moving, radii[i], bases[i])
            shunts.append(shunt)
            lane = lax.broadcasted_iota(jnp.int32, hot.shape, 1)
            last = lane == width - 1
            rise = jnp.where(last, 0.0, pltpu.roll(hot, width - 1, 1) - hot)
            ahead[i, here, :] = jnp.where(
                last, 0.0, radii[i] * axial_weight + (radii[i] * flow_weight) * moving
            )
            given[i, here, :] = radii[i] * goal[i, here, :]
            factor[i, here, :] = slope_weight * rise - (2.0 * heat_weight) * drag
        ratios, lefts, rights, ports = ladder(shunts, links, inverse_links)
        for i in range(rows):
            ratio[i, here, :] = ratios[i] if i < rows - 1 else jnp.zeros_like(hot)
            left_map[i, here, :] = lefts[i]
            right_map[i, here, :] = rights[i]
        for plane, port in enumerate(ports):
            put_tiles(condensed, group, plane, port)


def edge_kernel(heat, deform, flux, goal, old, low_edge, high_edge, held, ready):
    rows, azimuths, width = heat.shape
    ends = ((0, 1, low_edge), (azimuths - 1, azimuths - 2, high_edge))
    copies = []
    for e, (at, inner, _) in enumerate(ends):
        for k, (source, line) in enumerate(
            ((heat, at), (deform, at), (flux, at), (goal, at), (old, at), (old, inner))
        ):
            copy = pltpu.make_async_copy(source.at[:, line, :], held.at[e, k], ready.at[e, k])
            copy.start()
            copies.append(copy)
    total = rows * lax.axis_size("rad")
    first = (lax.axis_index("rad") * rows).astype(F32)
    row = lax.broadcasted_iota(jnp.int32, (rows, width), 0).astype(F32)
    radius = 1.0 + (first + (row + 0.5)) * (1.0 / total)
    base = 2.0 * azimuth_weight / (radius * radius) + (mass_weight + 2.0 * axial_weight)
    quarter = azimuth_weight / radius
    for e, (_, _, out) in enumerate(ends):
        for copy in copies[6 * e : 6 * e + 6]:
            copy.wait()
        hot, size, moving, given, centre, beside = [held[e, k] for k in range(6)]
        _, shunt = shunt_of(hot, size, moving, radius, base)
        out[0] = shunt
        out[1] = radius * explicit(centre, moving, given) + quarter * beside
        out[2] = centre


def explicit(centre, moving, given):
    after = lane_next(centre)
    return (
        given
        + axial_weight * (lane_prev(centre) + after)
        + flow_weight * moving * after
        + mass_weight * centre
    )


def place(padded, group, i, value):
    for t in range(value.shape[1] // LANE):
        padded[i, t, pl.ds((group + 1) * SUB, SUB), :] = value[:, t * LANE : (t + 1) * LANE]


def place_row(padded, at, i, value):
    for t in range(value.shape[1] // LANE):
        padded[i, t, at : at + 1, :] = value[:, t * LANE : (t + 1) * LANE]


def sources(group, padded, ahead, given, behind, radii, quarter):
    rows, tiles = padded.shape[:2]
    here = pl.ds(group * SUB, SUB)

    def lines(i, shift):
        at = pl.ds((group + 1) * SUB + shift, SUB)
        return jnp.concatenate([padded[i, t, at, :] for t in range(tiles)], axis=1)

    out = []
    for i in range(rows):
        centre = lines(i, 0)
        width = centre.shape[1]
        value = given[i, here, :] + ahead[i, here, :] * pltpu.roll(centre, width - 1, 1)
        value = value + behind[i] * pltpu.roll(centre, 1, 1)
        value = value + (radii[i] * mass_weight) * centre
        out.append(value + quarter[i] * (lines(i, -1) + lines(i, 1)))
    return out


def substitute(source, ratios, inverse_links):
    rows = len(source)
    currents = [source[0]]
    for i in range(1, rows):
        currents.append(source[i] + ratios[i - 1] * currents[-1])
    value = jnp.zeros_like(source[0])
    values = [value]
    for i in range(rows - 2, -1, -1):
        value = ratios[i] * (currents[i] * inverse_links[i + 1] + value)
        values.append(value)
    return values[::-1], currents[-1]


def local_solve(group, source, ratio, inverse_links, particular):
    rows = len(source)
    here = pl.ds(group * SUB, SUB)
    ratios = [ratio[i, here, :] for i in range(rows - 1)]
    values, outer = substitute(source, ratios, inverse_links)
    for i in range(rows):
        particular[i, here, :] = values[i]
    return values[0], outer


def tables(rows, width):
    links, radii = geometry(rows)
    inverse_links = [wide(1.0 / splat(link), width) for link in links]
    quarter = [wide(azimuth_weight / splat(radius), width) for radius in radii]
    first = lax.broadcasted_iota(jnp.int32, (1, width), 1) == 0
    behind = [jnp.where(first, 0.0, radius * axial_weight) for radius in radii]
    return links, radii, inverse_links, quarter, behind


def first_kernel(old, ahead, given, ratio, particular, ports, padded):
    rows, azimuths, width = old.shape
    links, radii, inverse_links, quarter, behind = tables(rows, width)
    for i in range(rows):
        place_row(padded, SUB - 1, i, jnp.zeros((1, width), F32))
        place_row(padded, SUB + azimuths, i, jnp.zeros((1, width), F32))
        for group in range(azimuths // SUB):
            place(padded, group, i, old[i, pl.ds(group * SUB, SUB), :])
    for group in range(azimuths // SUB):
        source = sources(group, padded, ahead, given, behind, radii, quarter)
        inner, outer = local_solve(group, source, ratio, inverse_links, particular)
        put_tiles(ports, group, 0, links[0] * inner)
        put_tiles(ports, group, 1, outer)


def pair_of(below, above):
    return jnp.concatenate([below, above], axis=0)


def edge_rows(ref, i):
    last = ref.shape[1] - 1
    return pair_of(ref[i, 0:1, :], ref[i, last : last + 1, :])


def join_kernel(old, below, above, ratio, condensed, ports, message, outside):
    rows, azimuths, width = old.shape
    links, radii, inverse_links, quarter, _ = tables(rows, width)
    tiles = message.shape[0]
    per = width // LANE
    message[:, 0:3] = condensed[...]
    message[:, 3:5] = ports[...]
    message[:, 5] = jnp.ones((tiles, SUB, LANE), F32)

    shunts, source, added = [], [], []
    for i in range(rows):
        row = pl.ds(i, 1)
        shunts.append(pair_of(below[0, row, :], above[0, row, :]))
        source.append(pair_of(below[1, row, :], above[1, row, :]) + quarter[i] * edge_rows(old, i))
        added.append(quarter[i] * pair_of(below[2, row, :], above[2, row, :]))
    ratios, lefts, rights, extra = ladder(shunts, links, inverse_links)
    values, outer = substitute(source, ratios, inverse_links)
    changes, change = substitute(added, [edge_rows(ratio, i) for i in range(rows - 1)], inverse_links)
    for i in range(rows):
        for slot, item in enumerate((values, lefts, rights, changes)):
            outside[slot, i] = item[i]
    for e, (at, row) in enumerate(((0, 0), (tiles - per, SUB - 1))):
        for t in range(per):
            lanes = slice(t * LANE, (t + 1) * LANE)
            for plane, port in enumerate((*extra, links[0] * values[0], outer)):
                message[e * per + t, 5, plane : plane + 1, :] = port[e : e + 1, lanes]
            for plane, port in ((3, links[0] * changes[0]), (4, change)):
                message[at + t, plane, row : row + 1, :] = (
                    ports[at + t, plane - 3, row : row + 1, :] + port[e : e + 1, lanes]
                )


def reduced_solve(last_link, through, inner, pivot, left, right):
    segments = len(through)
    inverses, ratios, offsets = [], [], []
    for s in range(segments):
        diagonal = pivot[s] + (inner[s + 1] if s + 1 < segments else last_link)
        given = right[s] + (left[s + 1] if s + 1 < segments else 0.0)
        if s > 0:
            diagonal = diagonal - through[s] * ratios[-1]
            given = given + ratios[-1] * carried
        carried = given
        inverse = 1.0 / diagonal
        inverses.append(inverse)
        offsets.append(given * inverse)
        if s + 1 < segments:
            ratios.append(through[s + 1] * inverse)
    out = []
    for s in range(segments - 1, -1, -1):
        if s + 1 < segments:
            value = offsets[s] + ratios[s] * value
            green = inverses[s] + ratios[s] * ratios[s] * green
            rising = ratios[s] * rising
        else:
            value, green, rising = offsets[s], inverses[s], jnp.ones_like(offsets[s])
        out.append((value, green, rising))
    return out[::-1]


def reduced_kernel(rows, got, sent):
    segments = got.shape[0]
    last_link = 2.0 * radial_weight * rows * rows
    main = reduced_solve(last_link, *[[got[s, p] for s in range(segments)] for p in range(5)])
    extra = reduced_solve(
        last_link, *[[got[s, 5, p : p + 1, :] for s in range(segments)] for p in range(5)]
    )
    zero = jnp.zeros((SUB, LANE), F32)
    for plane in (0, 2):
        sent[0, plane] = zero
    for s in range(segments):
        sent[s, 5] = zero
    for s in range(segments):
        value, green, rising = main[s]
        sent[s, 1] = value
        sent[s, 3] = rising
        sent[s, 4] = green / rising
        sent[s, 5, 1:2, :] = extra[s][0]
        if s + 1 < segments:
            sent[s + 1, 0] = value
            sent[s + 1, 2] = rising
            sent[s + 1, 5, 0:1, :] = extra[s][0]


def third_kernel(
    before,
    left_map,
    right_map,
    outside,
    ahead,
    given,
    condensed,
    got,
    source,
    own,
    fall,
    padded,
):
    rows, azimuths, width = before.shape
    links, radii, inverse_links, quarter, behind = tables(rows, width)
    per = width // LANE
    groups = azimuths // SUB
    sub = lax.broadcasted_iota(jnp.int32, (SUB, width), 0)

    def beyond(end):
        return pair_of(
            *[
                jnp.concatenate([got[e * per + t, 5, end : end + 1, :] for t in range(per)], axis=1)
                for e in range(2)
            ]
        )

    left, right = beyond(0), beyond(1)
    for i in range(rows):
        halo = outside[0, i] + outside[1, i] * left + outside[2, i] * right
        place_row(padded, SUB - 1, i, halo[0:1, :])
        place_row(padded, SUB + azimuths, i, halo[1:2, :])
    for group in range(groups):
        here = pl.ds(group * SUB, SUB)
        left = tiles_of(got, group, 0, width)
        right = tiles_of(got, group, 1, width)
        for i in range(rows):
            value = before[i, here, :] + left_map[i, here, :] * left + right_map[i, here, :] * right
            if group == 0:
                value = value + jnp.where(sub == 0, outside[3, i, 0:1, :], 0.0)
            if group == groups - 1:
                value = value + jnp.where(sub == SUB - 1, outside[3, i, 1:2, :], 0.0)
            place(padded, group, i, value)
    for group in range(groups):
        here = pl.ds(group * SUB, SUB)
        values = sources(group, padded, ahead, given, behind, radii, quarter)
        inner = jnp.zeros((SUB, width), F32)
        outer = values[rows - 1]
        for i in range(rows):
            source[i, here, :] = values[i]
            if i < rows - 1:
                inner = inner + left_map[i, here, :] * values[i]
                outer = outer + right_map[i, here, :] * values[i]
        rise_left, rise_right, fall_right = [tiles_of(got, group, plane, width) for plane in (2, 3, 4)]
        through = tiles_of(condensed, group, 0, width)
        fall_left = (1.0 / through + rise_left * fall_right) / rise_right
        fall_left = jnp.where(lax.axis_index("rad") == 0, 0.0, fall_left)
        fall[here, :] = fall_left
        own[0, here, :] = rise_left * inner + rise_right * outer
        own[1, here, :] = fall_left * inner + fall_right * outer


def inner_kernel(source, ratio, particular):
    rows, azimuths, width = source.shape
    _, _, inverse_links, _, _ = tables(rows, width)
    for group in range(azimuths // SUB):
        here = pl.ds(group * SUB, SUB)
        values = [source[i, here, :] for i in range(rows)]
        local_solve(group, values, ratio, inverse_links, particular)


def gather_kernel(own, first, second, third, near, message_far, message_near):
    mine = lax.rem(lax.axis_index("rad"), GROUP)
    block = lax.div(lax.axis_index("rad"), GROUP)
    for group in range(own.shape[1] // SUB):
        here = pl.ds(group * SUB, SUB)
        upward, downward = own[0, here, :], own[1, here, :]
        lower, upper = jnp.zeros_like(upward), downward
        for flip, other in ((1, first), (2, second), (3, third)):
            up, down = other[0, here, :], other[1, here, :]
            upward = upward + up
            downward = downward + down
            below = (mine ^ flip) < mine
            lower = lower + jnp.where(below, up, 0.0)
            upper = upper + jnp.where(below, 0.0, down)
        near[0, here, :] = lower
        near[1, here, :] = upper
        for message, flip in ((message_far, 2), (message_near, 1)):
            message[here, :] = jnp.where((block ^ flip) > block, upward, downward)


def last_kernel(
    particular,
    left_map,
    right_map,
    factor,
    got,
    own,
    fall,
    near,
    first,
    second,
    third,
    result,
    sensitivity,
    result_out,
    sensitivity_out,
    done,
):
    rows, azimuths, width = particular.shape
    block = lax.div(lax.axis_index("rad"), GROUP)
    copies = []
    for group in range(azimuths // SUB):
        here = pl.ds(group * SUB, SUB)
        lower, upper = near[0, here, :], near[1, here, :]
        for flip, other in ((1, first), (2, second), (3, third)):
            item = other[here, :]
            below = (block ^ flip) < block
            lower = lower + jnp.where(below, item, 0.0)
            upper = upper + jnp.where(below, 0.0, item)
        left = fall[here, :] * lower + tiles_of(got, group, 2, width) * upper
        right = (
            tiles_of(got, group, 4, width) * (lower + own[0, here, :])
            + tiles_of(got, group, 3, width) * (upper - own[1, here, :])
        )
        for i in range(rows):
            value = particular[i, here, :] + left_map[i, here, :] * left + right_map[i, here, :] * right
            result_out[i, here, :] = value
            sensitivity_out[i, here, :] = value * factor[i, here, :]
            piece = rows // 2 if group == azimuths // SUB - 1 else rows
            if (i + 1) % piece:
                continue
            part = pl.ds(i + 1 - piece, piece)
            for k, (source, target) in enumerate(
                ((result_out, result), (sensitivity_out, sensitivity))
            ):
                copy = pltpu.make_async_copy(
                    source.at[part, here, :], target.at[part, here, :], done.at[group, i // piece, k]
                )
                copy.start()
                copies.append(copy)
    for copy in copies:
        copy.wait()


def call(kernel, outs, *args, flops=1_000_000, remote=(), remote_outs=False, scratch=(), room=24):
    moved = sum(4 * a.size for a in args) + sum(4 * o.size for o in outs)
    near, away = pl.BlockSpec(memory_space=pltpu.VMEM), pl.BlockSpec(memory_space=pltpu.HBM)
    return pl.pallas_call(
        kernel,
        out_shape=outs,
        in_specs=[away if k in remote else near for k in range(len(args))],
        out_specs=tuple([away if remote_outs else near] * len(outs)),
        scratch_shapes=list(scratch),
        compiler_params=pltpu.CompilerParams(vmem_limit_bytes=int(room * 2**20)),
        cost_estimate=pl.CostEstimate(flops=flops, bytes_accessed=moved, transcendentals=0),
    )(*args)


def swap_edges(low_edge, high_edge):
    count = lax.axis_size("azi")
    below = lax.ppermute(high_edge, "azi", [(i, (i + 1) % count) for i in range(count)])
    above = lax.ppermute(low_edge, "azi", [((i + 1) % count, i) for i in range(count)])
    return below, above


def flip_permute(value, flip):
    return lax.ppermute(value, "rad", [(i, i ^ flip) for i in range(lax.axis_size("rad"))])


def exchange(value):
    return lax.all_to_all(value, "rad", 0, 0, tiled=True)


def body(heat, deform, flux, goal, start):
    rows, azimuths, width = heat.shape
    segments = lax.axis_size("rad")
    groups = azimuths // SUB
    tiles = azimuths * width // (SUB * LANE)
    block = jax.ShapeDtypeStruct((rows, azimuths, width), F32)
    pair = jax.ShapeDtypeStruct((2, azimuths, width), F32)
    edge = jax.ShapeDtypeStruct((3, rows, width), F32)
    held = pltpu.VMEM((rows, azimuths, width), F32)
    padded = pltpu.VMEM((rows, width // LANE, azimuths + 2 * SUB, LANE), F32)

    def planes(count):
        return jax.ShapeDtypeStruct((tiles, count, SUB, LANE), F32)

    edges = call(
        edge_kernel,
        (edge, edge),
        heat,
        deform,
        flux,
        goal,
        start,
        remote=range(5),
        room=53,
        scratch=(pltpu.VMEM((2, 6, rows, width), F32), pltpu.SemaphoreType.DMA((2, 6))),
    )
    below, above = swap_edges(*edges)
    ratio, left_map, right_map, factor, ahead, given, condensed = call(
        matrix_kernel,
        (block, block, block, block, block, block, planes(3)),
        heat,
        deform,
        flux,
        goal,
        flops=20_000_000,
    )
    particular, ports = call(
        first_kernel, (block, planes(2)), start, ahead, given, ratio, scratch=(padded,)
    )
    message, outside = call(
        join_kernel,
        (planes(6), jax.ShapeDtypeStruct((4, rows, 2, width), F32)),
        start,
        below,
        above,
        ratio,
        condensed,
        ports,
    )
    sent = call(
        lambda got, sent: reduced_kernel(rows, got, sent),
        (jax.ShapeDtypeStruct((segments, 6, SUB, LANE), F32),),
        exchange(message),
    )[0]
    got = exchange(sent)
    source, own, fall = call(
        third_kernel,
        (block, pair, jax.ShapeDtypeStruct((azimuths, width), F32)),
        particular,
        left_map,
        right_map,
        outside,
        ahead,
        given,
        condensed,
        got,
        scratch=(padded,),
    )
    (particular,) = call(inner_kernel, (block,), source, ratio)
    others = [flip_permute(own, flip) for flip in (1, 2, 3)]
    plane = jax.ShapeDtypeStruct((azimuths, width), F32)
    near, message_far, message_near = call(gather_kernel, (pair, plane, plane), own, *others)
    messages = (message_near, message_far, message_far)
    far = [flip_permute(item, flip * GROUP) for flip, item in zip((1, 2, 3), messages)]
    return call(
        last_kernel,
        (block, block),
        particular,
        left_map,
        right_map,
        factor,
        got,
        own,
        fall,
        near,
        *far,
        remote_outs=True,
        scratch=(held, held, pltpu.SemaphoreType.DMA((groups, 2, 2))),
    )


def solution(mesh):
    spec = P("rad", "azi", None)
    return jax.shard_map(
        body, mesh=mesh, in_specs=(spec,) * 5, out_specs=(spec, spec), check_vma=False
    )
```

```python
import jax
import jax.numpy as jnp
from jax import lax
from jax.experimental import pallas as pl
from jax.experimental.pallas import tpu as pltpu
from jax.sharding import PartitionSpec as P

radial_weight = 8.0
azimuth_weight = 0.25
axial_weight = 0.25
flow_weight = 0.5
mass_weight = 1.0
heat_weight = 0.25
arrhenius_exponent = 2.0
slope_weight = 2.0

SUB, LANE = 8, 128
GROUP = 4
F32 = jnp.float32


def geometry(rows):
    total = rows * lax.axis_size("rad")
    stiffness = radial_weight * rows * rows
    first = (lax.axis_index("rad") * rows).astype(F32)
    links = [stiffness + (stiffness / total) * (first + float(i)) for i in range(rows + 1)]
    radii = [1.0 + (first + (i + 0.5)) * (1.0 / total) for i in range(rows)]
    return links, radii


def splat(scalar):
    return jnp.full((1, LANE), scalar, F32)


def wide(row, width):
    return jnp.concatenate([row] * (width // LANE), axis=1)


def tiles_of(ref, group, plane, width):
    per = width // LANE
    return jnp.concatenate([ref[group * per + t, plane] for t in range(per)], axis=1)


def put_tiles(ref, group, plane, value):
    per = value.shape[1] // LANE
    for t in range(per):
        ref[group * per + t, plane] = value[:, t * LANE : (t + 1) * LANE]


def lane_next(value):
    width = value.shape[1]
    lane = lax.broadcasted_iota(jnp.int32, value.shape, 1)
    return jnp.where(lane == width - 1, 0.0, pltpu.roll(value, width - 1, 1))


def lane_prev(value):
    lane = lax.broadcasted_iota(jnp.int32, value.shape, 1)
    return jnp.where(lane == 0, 0.0, pltpu.roll(value, 1, 1))


def shunt_of(hot, size, drag_flux, radius, base):
    drag = jnp.exp(-arrhenius_exponent * (hot - 1.0)) * size
    heating = (heat_weight * arrhenius_exponent) * (drag * size)
    return drag, radius * (base + flow_weight * drag_flux + heating)


def ladder(shunts, links, inverse_links):
    rows = len(shunts)
    ratios, lefts = [], []
    through = jnp.full(shunts[0].shape, links[0], F32)
    pivot = shunts[0] + links[0]
    for i in range(rows):
        if i > 0:
            pivot = shunts[i] + ratios[-1] * pivot
        lefts.append(through)
        if i < rows - 1:
            step = links[i + 1] / (links[i + 1] + pivot)
            ratios.append(step)
            through = step * through
    from_left = jnp.zeros_like(through)
    from_right = jnp.ones_like(through)
    left_maps, right_maps = [from_left], [from_right]
    for i in range(rows - 2, -1, -1):
        from_left = ratios[i] * (lefts[i] * inverse_links[i + 1] + from_left)
        from_right = ratios[i] * from_right
        left_maps.append(from_left)
        right_maps.append(from_right)
    inner = links[0] * (1.0 - from_left)
    return ratios, left_maps[::-1], right_maps[::-1], (through, inner, pivot)


def base_shunts(radii):
    out = []
    for radius in radii:
        r = splat(radius)
        out.append(2.0 * azimuth_weight / (r * r) + (mass_weight + 2.0 * axial_weight))
    return out


def matrix_kernel(
    heat,
    deform,
    flux,
    goal,
    ratio,
    left_map,
    right_map,
    factor,
    ahead,
    given,
    condensed,
):
    rows, azimuths, width = heat.shape
    links, radii = geometry(rows)
    inverse_links = [wide(1.0 / splat(link), width) for link in links]
    bases = [wide(base, width) for base in base_shunts(radii)]
    for group in range(azimuths // SUB):
        here = pl.ds(group * SUB, SUB)
        shunts = []
        for i in range(rows):
            hot = heat[i, here, :]
            moving = flux[i, here, :]
            drag, shunt = shunt_of(hot, deform[i, here, :], moving, radii[i], bases[i])
            shunts.append(shunt)
            lane = lax.broadcasted_iota(jnp.int32, hot.shape, 1)
            last = lane == width - 1
            rise = jnp.where(last, 0.0, pltpu.roll(hot, width - 1, 1) - hot)
            ahead[i, here, :] = jnp.where(
                last, 0.0, radii[i] * axial_weight + (radii[i] * flow_weight) * moving
            )
            given[i, here, :] = radii[i] * goal[i, here, :]
            factor[i, here, :] = slope_weight * rise - (2.0 * heat_weight) * drag
        ratios, lefts, rights, ports = ladder(shunts, links, inverse_links)
        for i in range(rows):
            ratio[i, here, :] = ratios[i] if i < rows - 1 else jnp.zeros_like(hot)
            left_map[i, here, :] = lefts[i]
            right_map[i, here, :] = rights[i]
        for plane, port in enumerate(ports):
            put_tiles(condensed, group, plane, port)


def edge_kernel(heat, deform, flux, goal, old, low_edge, high_edge, held, ready):
    rows, azimuths, width = heat.shape
    ends = ((0, 1, low_edge), (azimuths - 1, azimuths - 2, high_edge))
    copies = []
    for e, (at, inner, _) in enumerate(ends):
        for k, (source, line) in enumerate(
            ((heat, at), (deform, at), (flux, at), (goal, at), (old, at), (old, inner))
        ):
            copy = pltpu.make_async_copy(source.at[:, line, :], held.at[e, k], ready.at[e, k])
            copy.start()
            copies.append(copy)
    total = rows * lax.axis_size("rad")
    first = (lax.axis_index("rad") * rows).astype(F32)
    row = lax.broadcasted_iota(jnp.int32, (rows, width), 0).astype(F32)
    radius = 1.0 + (first + (row + 0.5)) * (1.0 / total)
    base = 2.0 * azimuth_weight / (radius * radius) + (mass_weight + 2.0 * axial_weight)
    quarter = azimuth_weight / radius
    for e, (_, _, out) in enumerate(ends):
        for copy in copies[6 * e : 6 * e + 6]:
            copy.wait()
        hot, size, moving, given, centre, beside = [held[e, k] for k in range(6)]
        _, shunt = shunt_of(hot, size, moving, radius, base)
        out[0] = shunt
        out[1] = radius * explicit(centre, moving, given) + quarter * beside
        out[2] = centre


def explicit(centre, moving, given):
    after = lane_next(centre)
    return (
        given
        + axial_weight * (lane_prev(centre) + after)
        + flow_weight * moving * after
        + mass_weight * centre
    )


def place(padded, group, i, value):
    for t in range(value.shape[1] // LANE):
        padded[i, t, pl.ds((group + 1) * SUB, SUB), :] = value[:, t * LANE : (t + 1) * LANE]


def place_row(padded, at, i, value):
    for t in range(value.shape[1] // LANE):
        padded[i, t, at : at + 1, :] = value[:, t * LANE : (t + 1) * LANE]


def sources(group, padded, ahead, given, behind, radii, quarter):
    rows, tiles = padded.shape[:2]
    here = pl.ds(group * SUB, SUB)

    def lines(i, shift):
        at = pl.ds((group + 1) * SUB + shift, SUB)
        return jnp.concatenate([padded[i, t, at, :] for t in range(tiles)], axis=1)

    out = []
    for i in range(rows):
        centre = lines(i, 0)
        width = centre.shape[1]
        value = given[i, here, :] + ahead[i, here, :] * pltpu.roll(centre, width - 1, 1)
        value = value + behind[i] * pltpu.roll(centre, 1, 1)
        value = value + (radii[i] * mass_weight) * centre
        out.append(value + quarter[i] * (lines(i, -1) + lines(i, 1)))
    return out


def substitute(source, ratios, inverse_links):
    rows = len(source)
    currents = [source[0]]
    for i in range(1, rows):
        currents.append(source[i] + ratios[i - 1] * currents[-1])
    value = jnp.zeros_like(source[0])
    values = [value]
    for i in range(rows - 2, -1, -1):
        value = ratios[i] * (currents[i] * inverse_links[i + 1] + value)
        values.append(value)
    return values[::-1], currents[-1]


def local_solve(group, source, ratio, inverse_links, particular):
    rows = len(source)
    here = pl.ds(group * SUB, SUB)
    ratios = [ratio[i, here, :] for i in range(rows - 1)]
    values, outer = substitute(source, ratios, inverse_links)
    for i in range(rows):
        particular[i, here, :] = values[i]
    return values[0], outer


def tables(rows, width):
    links, radii = geometry(rows)
    inverse_links = [wide(1.0 / splat(link), width) for link in links]
    quarter = [wide(azimuth_weight / splat(radius), width) for radius in radii]
    first = lax.broadcasted_iota(jnp.int32, (1, width), 1) == 0
    behind = [jnp.where(first, 0.0, radius * axial_weight) for radius in radii]
    return links, radii, inverse_links, quarter, behind


def first_kernel(old, ahead, given, ratio, particular, ports, padded):
    rows, azimuths, width = old.shape
    links, radii, inverse_links, quarter, behind = tables(rows, width)
    for i in range(rows):
        place_row(padded, SUB - 1, i, jnp.zeros((1, width), F32))
        place_row(padded, SUB + azimuths, i, jnp.zeros((1, width), F32))
        for group in range(azimuths // SUB):
            place(padded, group, i, old[i, pl.ds(group * SUB, SUB), :])
    for group in range(azimuths // SUB):
        source = sources(group, padded, ahead, given, behind, radii, quarter)
        inner, outer = local_solve(group, source, ratio, inverse_links, particular)
        put_tiles(ports, group, 0, links[0] * inner)
        put_tiles(ports, group, 1, outer)


def pair_of(below, above):
    return jnp.concatenate([below, above], axis=0)


def edge_rows(ref, i):
    last = ref.shape[1] - 1
    return pair_of(ref[i, 0:1, :], ref[i, last : last + 1, :])


def join_kernel(old, below, above, ratio, condensed, ports, message, outside):
    rows, azimuths, width = old.shape
    links, radii, inverse_links, quarter, _ = tables(rows, width)
    tiles = message.shape[0]
    per = width // LANE
    message[:, 0:3] = condensed[...]
    message[:, 3:5] = ports[...]
    message[:, 5] = jnp.ones((tiles, SUB, LANE), F32)

    shunts, source, added = [], [], []
    for i in range(rows):
        row = pl.ds(i, 1)
        shunts.append(pair_of(below[0, row, :], above[0, row, :]))
        source.append(pair_of(below[1, row, :], above[1, row, :]) + quarter[i] * edge_rows(old, i))
        added.append(quarter[i] * pair_of(below[2, row, :], above[2, row, :]))
    ratios, lefts, rights, extra = ladder(shunts, links, inverse_links)
    values, outer = substitute(source, ratios, inverse_links)
    changes, change = substitute(added, [edge_rows(ratio, i) for i in range(rows - 1)], inverse_links)
    for i in range(rows):
        for slot, item in enumerate((values, lefts, rights, changes)):
            outside[slot, i] = item[i]
    for e, (at, row) in enumerate(((0, 0), (tiles - per, SUB - 1))):
        for t in range(per):
            lanes = slice(t * LANE, (t + 1) * LANE)
            for plane, port in enumerate((*extra, links[0] * values[0], outer)):
                message[e * per + t, 5, plane : plane + 1, :] = port[e : e + 1, lanes]
            for plane, port in ((3, links[0] * changes[0]), (4, change)):
                message[at + t, plane, row : row + 1, :] = (
                    ports[at + t, plane - 3, row : row + 1, :] + port[e : e + 1, lanes]
                )


def reduced_solve(last_link, through, inner, pivot, left, right):
    segments = len(through)
    inverses, ratios, offsets = [], [], []
    for s in range(segments):
        diagonal = pivot[s] + (inner[s + 1] if s + 1 < segments else last_link)
        given = right[s] + (left[s + 1] if s + 1 < segments else 0.0)
        if s > 0:
            diagonal = diagonal - through[s] * ratios[-1]
            given = given + ratios[-1] * carried
        carried = given
        inverse = 1.0 / diagonal
        inverses.append(inverse)
        offsets.append(given * inverse)
        if s + 1 < segments:
            ratios.append(through[s + 1] * inverse)
    out = []
    for s in range(segments - 1, -1, -1):
        if s + 1 < segments:
            value = offsets[s] + ratios[s] * value
            green = inverses[s] + ratios[s] * ratios[s] * green
            rising = ratios[s] * rising
        else:
            value, green, rising = offsets[s], inverses[s], jnp.ones_like(offsets[s])
        out.append((value, green, rising))
    return out[::-1]


def reduced_kernel(rows, got, sent):
    segments = got.shape[0]
    last_link = 2.0 * radial_weight * rows * rows
    main = reduced_solve(last_link, *[[got[s, p] for s in range(segments)] for p in range(5)])
    extra = reduced_solve(
        last_link, *[[got[s, 5, p : p + 1, :] for s in range(segments)] for p in range(5)]
    )
    zero = jnp.zeros((SUB, LANE), F32)
    for plane in (0, 2):
        sent[0, plane] = zero
    for s in range(segments):
        sent[s, 5] = zero
    for s in range(segments):
        value, green, rising = main[s]
        sent[s, 1] = value
        sent[s, 3] = rising
        sent[s, 4] = green / rising
        sent[s, 5, 1:2, :] = extra[s][0]
        if s + 1 < segments:
            sent[s + 1, 0] = value
            sent[s + 1, 2] = rising
            sent[s + 1, 5, 0:1, :] = extra[s][0]


def third_kernel(
    before,
    left_map,
    right_map,
    outside,
    ahead,
    given,
    ratio,
    condensed,
    got,
    particular,
    own,
    fall,
    padded,
):
    rows, azimuths, width = before.shape
    links, radii, inverse_links, quarter, behind = tables(rows, width)
    per = width // LANE
    groups = azimuths // SUB
    sub = lax.broadcasted_iota(jnp.int32, (SUB, width), 0)

    def beyond(end):
        return pair_of(
            *[
                jnp.concatenate([got[e * per + t, 5, end : end + 1, :] for t in range(per)], axis=1)
                for e in range(2)
            ]
        )

    left, right = beyond(0), beyond(1)
    for i in range(rows):
        halo = outside[0, i] + outside[1, i] * left + outside[2, i] * right
        place_row(padded, SUB - 1, i, halo[0:1, :])
        place_row(padded, SUB + azimuths, i, halo[1:2, :])
    for group in range(groups):
        here = pl.ds(group * SUB, SUB)
        left = tiles_of(got, group, 0, width)
        right = tiles_of(got, group, 1, width)
        for i in range(rows):
            value = before[i, here, :] + left_map[i, here, :] * left + right_map[i, here, :] * right
            if group == 0:
                value = value + jnp.where(sub == 0, outside[3, i, 0:1, :], 0.0)
            if group == groups - 1:
                value = value + jnp.where(sub == SUB - 1, outside[3, i, 1:2, :], 0.0)
            place(padded, group, i, value)
    for group in range(groups):
        here = pl.ds(group * SUB, SUB)
        source = sources(group, padded, ahead, given, behind, radii, quarter)
        inner, outer = local_solve(group, source, ratio, inverse_links, particular)
        inner = links[0] * inner
        rise_left, rise_right, fall_right = [tiles_of(got, group, plane, width) for plane in (2, 3, 4)]
        through = tiles_of(condensed, group, 0, width)
        fall_left = (1.0 / through + rise_left * fall_right) / rise_right
        fall_left = jnp.where(lax.axis_index("rad") == 0, 0.0, fall_left)
        fall[here, :] = fall_left
        own[0, here, :] = rise_left * inner + rise_right * outer
        own[1, here, :] = fall_left * inner + fall_right * outer


def gather_kernel(own, first, second, third, near, message_far, message_near):
    mine = lax.rem(lax.axis_index("rad"), GROUP)
    block = lax.div(lax.axis_index("rad"), GROUP)
    for group in range(own.shape[1] // SUB):
        here = pl.ds(group * SUB, SUB)
        upward, downward = own[0, here, :], own[1, here, :]
        lower, upper = jnp.zeros_like(upward), downward
        for flip, other in ((1, first), (2, second), (3, third)):
            up, down = other[0, here, :], other[1, here, :]
            upward = upward + up
            downward = downward + down
            below = (mine ^ flip) < mine
            lower = lower + jnp.where(below, up, 0.0)
            upper = upper + jnp.where(below, 0.0, down)
        near[0, here, :] = lower
        near[1, here, :] = upper
        for message, flip in ((message_far, 2), (message_near, 1)):
            message[here, :] = jnp.where((block ^ flip) > block, upward, downward)


def last_kernel(
    particular,
    left_map,
    right_map,
    factor,
    got,
    own,
    fall,
    near,
    first,
    second,
    third,
    result,
    sensitivity,
    result_out,
    sensitivity_out,
    done,
):
    rows, azimuths, width = particular.shape
    block = lax.div(lax.axis_index("rad"), GROUP)
    copies = []
    for group in range(azimuths // SUB):
        here = pl.ds(group * SUB, SUB)
        lower, upper = near[0, here, :], near[1, here, :]
        for flip, other in ((1, first), (2, second), (3, third)):
            item = other[here, :]
            below = (block ^ flip) < block
            lower = lower + jnp.where(below, item, 0.0)
            upper = upper + jnp.where(below, 0.0, item)
        left = fall[here, :] * lower + tiles_of(got, group, 2, width) * upper
        right = (
            tiles_of(got, group, 4, width) * (lower + own[0, here, :])
            + tiles_of(got, group, 3, width) * (upper - own[1, here, :])
        )
        for i in range(rows):
            value = particular[i, here, :] + left_map[i, here, :] * left + right_map[i, here, :] * right
            result_out[i, here, :] = value
            sensitivity_out[i, here, :] = value * factor[i, here, :]
            piece = rows // 2 if group == azimuths // SUB - 1 else rows
            if (i + 1) % piece:
                continue
            part = pl.ds(i + 1 - piece, piece)
            for k, (source, target) in enumerate(
                ((result_out, result), (sensitivity_out, sensitivity))
            ):
                copy = pltpu.make_async_copy(
                    source.at[part, here, :], target.at[part, here, :], done.at[group, i // piece, k]
                )
                copy.start()
                copies.append(copy)
    for copy in copies:
        copy.wait()


def call(kernel, outs, *args, flops=1_000_000, remote=(), remote_outs=False, scratch=(), room=24):
    moved = sum(4 * a.size for a in args) + sum(4 * o.size for o in outs)
    near, away = pl.BlockSpec(memory_space=pltpu.VMEM), pl.BlockSpec(memory_space=pltpu.HBM)
    return pl.pallas_call(
        kernel,
        out_shape=outs,
        in_specs=[away if k in remote else near for k in range(len(args))],
        out_specs=tuple([away if remote_outs else near] * len(outs)),
        scratch_shapes=list(scratch),
        compiler_params=pltpu.CompilerParams(vmem_limit_bytes=int(room * 2**20)),
        cost_estimate=pl.CostEstimate(flops=flops, bytes_accessed=moved, transcendentals=0),
    )(*args)


def swap_edges(low_edge, high_edge):
    count = lax.axis_size("azi")
    below = lax.ppermute(high_edge, "azi", [(i, (i + 1) % count) for i in range(count)])
    above = lax.ppermute(low_edge, "azi", [((i + 1) % count, i) for i in range(count)])
    return below, above


def flip_permute(value, flip):
    return lax.ppermute(value, "rad", [(i, i ^ flip) for i in range(lax.axis_size("rad"))])


def exchange(value):
    return lax.all_to_all(value, "rad", 0, 0, tiled=True)


def body(heat, deform, flux, goal, start):
    rows, azimuths, width = heat.shape
    segments = lax.axis_size("rad")
    groups = azimuths // SUB
    tiles = azimuths * width // (SUB * LANE)
    block = jax.ShapeDtypeStruct((rows, azimuths, width), F32)
    pair = jax.ShapeDtypeStruct((2, azimuths, width), F32)
    edge = jax.ShapeDtypeStruct((3, rows, width), F32)
    held = pltpu.VMEM((rows, azimuths, width), F32)
    padded = pltpu.VMEM((rows, width // LANE, azimuths + 2 * SUB, LANE), F32)

    def planes(count):
        return jax.ShapeDtypeStruct((tiles, count, SUB, LANE), F32)

    edges = call(
        edge_kernel,
        (edge, edge),
        heat,
        deform,
        flux,
        goal,
        start,
        remote=range(5),
        room=53,
        scratch=(pltpu.VMEM((2, 6, rows, width), F32), pltpu.SemaphoreType.DMA((2, 6))),
    )
    below, above = swap_edges(*edges)
    ratio, left_map, right_map, factor, ahead, given, condensed = call(
        matrix_kernel,
        (block, block, block, block, block, block, planes(3)),
        heat,
        deform,
        flux,
        goal,
        flops=20_000_000,
    )
    particular, ports = call(
        first_kernel, (block, planes(2)), start, ahead, given, ratio, scratch=(padded,)
    )
    message, outside = call(
        join_kernel,
        (planes(6), jax.ShapeDtypeStruct((4, rows, 2, width), F32)),
        start,
        below,
        above,
        ratio,
        condensed,
        ports,
    )
    sent = call(
        lambda got, sent: reduced_kernel(rows, got, sent),
        (jax.ShapeDtypeStruct((segments, 6, SUB, LANE), F32),),
        exchange(message),
    )[0]
    got = exchange(sent)
    particular, own, fall = call(
        third_kernel,
        (block, pair, jax.ShapeDtypeStruct((azimuths, width), F32)),
        particular,
        left_map,
        right_map,
        outside,
        ahead,
        given,
        ratio,
        condensed,
        got,
        scratch=(padded,),
    )
    others = [flip_permute(own, flip) for flip in (1, 2, 3)]
    plane = jax.ShapeDtypeStruct((azimuths, width), F32)
    near, message_far, message_near = call(gather_kernel, (pair, plane, plane), own, *others)
    messages = (message_near, message_far, message_far)
    far = [flip_permute(item, flip * GROUP) for flip, item in zip((1, 2, 3), messages)]
    return call(
        last_kernel,
        (block, block),
        particular,
        left_map,
        right_map,
        factor,
        got,
        own,
        fall,
        near,
        *far,
        remote_outs=True,
        scratch=(held, held, pltpu.SemaphoreType.DMA((groups, 2, 2))),
    )


def solution(mesh):
    spec = P("rad", "azi", None)
    return jax.shard_map(
        body, mesh=mesh, in_specs=(spec,) * 5, out_specs=(spec, spec), check_vma=False
    )
```
